256 devices in a mesh: ctx: 32 (over z, x), kvh: 8 (over y, core).
Axes of the slice: x: 4, y: 4, z: 8, core: 2. Of those that a mesh axis runs over, the one named last changes fastest.
Arguments:
- queries: bfloat16 [8, 2048, 1024], P('kvh', 'ctx'), may hold values from -15 to 15
- span_kv: bfloat16 [2, 8, 2048, 128], P(None, 'kvh', 'ctx'), may hold values from -6 to 6
- cache_kv: bfloat16 [2, 8, 262144, 128], P(None, 'kvh', 'ctx'), may hold values from -6 to 6
- choices: int32 [8, 2048, 3], P('kvh'), may hold values from 0 to 63, all different within a row; in each aligned block of 64 rows (0 to 63, 64 to 127, ..., all dimensions but the last counted through in order) at most 4 rows name the same one
- block_home: int32 [64], replicated, may hold values from 0 to 63, each once
- out_weight: bfloat16 [8192, 4096], P('kvh'), may hold values from -0.0625 to 0.0625
Outputs:
- attended: bfloat16 [8, 2048, 1024], P('kvh', 'ctx')
- projected: bfloat16 [2048, 4096], P(('ctx', 'kvh'))
The draws below stay inside these ranges and needn't reach their ends.
Inputs may be any that keep to these rules, and one draw needn't show every extreme that they name: `choices`: each row names 3 different blocks. Among the rows k * 64 to (k + 1) * 64 - 1 of one KV head, at most 4 rows name the same block. `block_home`: each storage slot holds exactly one block.
All inputs are finite; a program needn't handle non-finite values.
Results may differ from the reference program's by a relative error of at most 0.019.
Values may be sent and summed in bfloat16 or wider, within the bound.
A program may use at most 128 MiB of HBM per device.

```python
import math
import jax
import jax.numpy as jnp
import numpy as np
from jax import lax

HEAD_DIM = 128
GROUP = 8
OUT_COLS = 4096
BLOCK_LEN = 4096
TOPK = 3
Q_DEV = 64
KV_HEADS = 8
BLOCKS = 64
SPAN = 2048
MOST = 4
N_CTX = 32


def draw_queries(key, part):
    key = jax.random.fold_in(key, 11)
    shape = (KV_HEADS, SPAN, GROUP * HEAD_DIM)
    values = jnp.clip(2.5 * jax.random.normal(key, shape, jnp.float32), -15.0, 15.0)
    return values.astype(jnp.bfloat16)


def draw_span_kv(key, part):
    key = jax.random.fold_in(key, 23)
    shape = (2, KV_HEADS, SPAN, HEAD_DIM)
    values = jnp.clip(jax.random.normal(key, shape, jnp.float32), -6.0, 6.0)
    return values.astype(jnp.bfloat16)


def draw_cache_kv(key, part):
    key = jax.random.fold_in(key, 37)
    shape = (2, KV_HEADS, BLOCKS * BLOCK_LEN, HEAD_DIM)
    values = jnp.clip(jax.random.normal(key, shape, jnp.float32), -6.0, 6.0)
    return values.astype(jnp.bfloat16)


def block_levels(rng, dims, shards, least, high):
    factor_of, own = 1.0, jax.random.fold_in(rng, 6)
    for dim, shards_of in shards:
        heights = jnp.exp(jax.random.uniform(jax.random.fold_in(own, dim), (shards_of,), jnp.float32, least / len(shards), high / len(shards)))
        factor_of = factor_of * jnp.repeat(heights, dims[dim] // shards_of).reshape([-1 if axis == dim else 1 for axis in range(len(dims))])
    return factor_of


def assign_block(key, own, number, rows, count, top, reach, lean):
    order = jax.random.permutation(key, count)
    heavy_load, common = portions_of(count, rows * top, reach, lean, True), portions_of(count, rows * top, reach, lean, False)
    places = jnp.arange(count)

    def named(sizes, rotation):
        used = int((sizes > 0).sum())
        fixed = max(1, used // 4)
        passed = fixed + (places - fixed + rotation * (used - fixed)) % max(1, count - fixed)
        return jnp.zeros((count,), jnp.int32).at[order[jnp.where(places < fixed, places, passed)]].set(jnp.asarray(sizes, jnp.int32))

    sizes = jnp.where(number % 4 == 0, named(heavy_load, number // 4), named(common, number - number // 4 - 1))
    mixed = jax.random.permutation(jax.random.fold_in(own, 3), count)
    giver, taker = mixed[0:count // 2 * 2:2], mixed[1:count // 2 * 2:2]
    slack = jnp.minimum(sizes[giver] - 1, reach - sizes[taker]) // 2
    slack = jnp.where((giver == order[0]) | (taker == order[0]) | (sizes[taker] == 0), 0, jnp.maximum(slack, 0))
    passed = jax.random.randint(jax.random.fold_in(own, 4), (count // 2,), 0, 1 << 20) % (slack + 1)
    sizes = sizes.at[giver].add(-passed).at[taker].add(passed)
    items = jnp.searchsorted(jnp.cumsum(sizes), jnp.arange(rows * top), side="right").astype(jnp.int32)
    grid = items.reshape(top, rows).T
    grid = grid[jax.random.permutation(jax.random.fold_in(own, 1), rows)]
    rotation = jax.random.randint(jax.random.fold_in(own, 2), (rows, 1), 0, top)
    return jnp.take_along_axis(grid, (jnp.arange(top)[None, :] + rotation) % top, axis=1)


def portions_of(count, total, limit, slope, full):
    portions = [(1 << 20) // math.isqrt(rank ** slope) + 1 for rank in range(1, count + 1)]
    largest = limit if full else min(limit, max(-(-total // count), total * portions[0] // sum(portions)))
    least = 1 if total - largest >= count - 1 else 0
    given, surplus = [largest] + [least] * (count - 1), total - largest - least * (count - 1)
    while surplus > 0:
        free = [i for i in range(1, count) if given[i] < largest] or [i for i in range(1, count) if given[i] < limit]
        whole, remaining = sum([portions[i] for i in free]), surplus
        for i in free:
            addition = min(limit - given[i], max(1, remaining * portions[i] // whole), surplus)
            given[i] = given[i] + addition
            surplus = surplus - addition
    return np.array(given)


def scatter_about(stream_key, dims, scale, most, shards=(), kind=jnp.bfloat16):
    factor_of = block_levels(stream_key, dims, shards, -0.22, 0.18) if shards else 1.0
    values = jax.random.normal(stream_key, dims, jnp.float32) * scale * factor_of
    return jnp.minimum(jnp.maximum(values, -most), most).astype(kind)


def setup_inputs(seed: int = 0) -> dict:
    keys = jax.random.split(jax.random.key(seed), 7)
    queries = draw_queries(jax.random.fold_in(keys[6], 71), 0)
    span_kv = draw_span_kv(jax.random.fold_in(keys[6], 71), 0)
    cache_kv = draw_cache_kv(jax.random.fold_in(keys[6], 71), 0)
    choices_keys = jax.random.split(jax.random.fold_in(keys[3], 1), KV_HEADS * SPAN // Q_DEV)
    choices_turns = jax.random.permutation(jax.random.fold_in(keys[3], 3), KV_HEADS * SPAN // Q_DEV)
    choices = jax.vmap(lambda own, number: assign_block(jax.random.fold_in(keys[3], 2), own, number, Q_DEV, BLOCKS, TOPK, MOST, 2))(choices_keys, choices_turns).reshape((KV_HEADS, SPAN, TOPK))
    block_home = jax.random.permutation(keys[4], BLOCKS).astype(jnp.int32)
    out_weight = scatter_about(keys[5], (KV_HEADS * GROUP * HEAD_DIM, OUT_COLS), (KV_HEADS * GROUP * HEAD_DIM) ** -0.5, 0.0625, ((0, 8),))
    return dict(queries=queries, span_kv=span_kv, cache_kv=cache_kv, choices=choices, block_home=block_home, out_weight=out_weight)


def block_attention(query_rows, key_rows, value_rows, score_scale, allowed):
    scores = lax.dot_general(query_rows, key_rows, (((1,), (1,)), ((), ())), preferred_element_type=jnp.float32) * score_scale
    if allowed is not None:
        scores = jnp.where(allowed, scores, -1e+30)
    peak_value = lax.optimization_barrier(jnp.max(scores, axis=1, keepdims=True))
    exponent = jnp.exp(scores - peak_value)
    totals = lax.optimization_barrier(jnp.sum(exponent, axis=1, keepdims=True))
    weights = exponent.astype(jnp.bfloat16)
    part_out = jnp.dot(weights, value_rows, preferred_element_type=jnp.float32) / totals
    return (part_out, (peak_value + jnp.log(totals))[:, 0])

def merge_parts(own_out, own_lse, far_out, far_lse):
    all_lse = jnp.concatenate([own_lse[:, None], far_lse], axis=1)
    all_out = jnp.concatenate([own_out[:, None], far_out.astype(jnp.float32)], axis=1)
    peak_value = lax.optimization_barrier(jnp.max(all_lse, axis=1, keepdims=True))
    factors = jnp.exp(all_lse - peak_value)
    return lax.optimization_barrier(jnp.sum(factors[..., None] * all_out, axis=1)) / lax.optimization_barrier(jnp.sum(factors, axis=1))[..., None]

def reference(queries, span_kv, cache_kv, choices, block_home, out_weight):
    score_scale = 1.0 / math.sqrt(HEAD_DIM)
    capacity = N_CTX * MOST
    positions = jnp.arange(SPAN, dtype=jnp.int32)
    allowed = positions[None, :] <= jnp.repeat(positions, GROUP)[:, None]

    def one_head(head_index):
        q_head = lax.dynamic_index_in_dim(queries, head_index, 0, keepdims=False)
        c_head = lax.dynamic_index_in_dim(choices, head_index, 0, keepdims=False)
        cache_head = lax.dynamic_index_in_dim(cache_kv, head_index, 1, keepdims=False)
        span_head = lax.dynamic_index_in_dim(span_kv, head_index, 1, keepdims=False)
        q_rows = q_head.reshape(SPAN * GROUP, HEAD_DIM)
        own_out, own_lse = block_attention(q_rows, span_head[0], span_head[1], score_scale, allowed)

        def per_block(carried, block_index):
            far_out, far_lse = carried
            matches = c_head == block_index
            chosen = jnp.any(matches, axis=1)
            ranking = jnp.argsort(jnp.where(chosen, 0, 1).astype(jnp.int32), stable=True).astype(jnp.int32)[:capacity]
            is_used = chosen[ranking]
            pick_pos = lax.optimization_barrier(jnp.sum(jnp.where(matches, jnp.arange(TOPK, dtype=jnp.int32)[None, :], 0), axis=1)).astype(jnp.int32)[ranking]
            row_start = (block_home[block_index] * BLOCK_LEN).astype(jnp.int32)
            block_kv = lax.dynamic_slice_in_dim(cache_head, row_start, BLOCK_LEN, 1)
            picked = q_head[ranking].reshape(capacity * GROUP, HEAD_DIM)
            part_out, part_lse = block_attention(picked, block_kv[0], block_kv[1], score_scale, None)
            target = jnp.where(is_used, ranking, SPAN).astype(jnp.int32)
            far_out = far_out.at[target, pick_pos].set(part_out.astype(jnp.bfloat16).reshape(capacity, GROUP, HEAD_DIM), mode='drop')
            far_lse = far_lse.at[target, pick_pos].set(part_lse.reshape(capacity, GROUP), mode='drop')
            return ((far_out, far_lse), None)
        initial = (jnp.zeros((SPAN, TOPK, GROUP, HEAD_DIM), jnp.bfloat16), jnp.zeros((SPAN, TOPK, GROUP), jnp.float32))
        (far_out, far_lse), _ = lax.scan(per_block, initial, jnp.arange(BLOCKS, dtype=jnp.int32))
        combined = merge_parts(own_out.reshape(SPAN, GROUP, HEAD_DIM), own_lse.reshape(SPAN, GROUP), far_out, far_lse)
        return combined.reshape(SPAN, GROUP * HEAD_DIM).astype(jnp.bfloat16)
    attended = lax.map(one_head, jnp.arange(KV_HEADS, dtype=jnp.int32))
    flattened = jnp.transpose(attended, (1, 0, 2)).reshape(SPAN, KV_HEADS * GROUP * HEAD_DIM)
    projected = jnp.dot(flattened, out_weight, preferred_element_type=jnp.float32).astype(jnp.bfloat16)
    return (attended, projected)
```

```python
import functools
import math

import jax
import jax.numpy as jnp
from jax import lax
from jax.experimental import pallas as pl
from jax.experimental.pallas import tpu as pltpu
from jax.sharding import PartitionSpec as P

MESH = pl.DeviceIdType.MESH
F32 = jnp.float32
BF16 = jnp.bfloat16

NZ, NX, NK = 8, 4, 8
N = NZ * NX
QD = 64
HD = 128
GR = 8
TOP = 3
MOST = 4
NB = 64
BL = 4096
JB = 2
COLS = 4096
TILES = 4
PT = N // TILES
RT = PT * GR * MOST
SCALE = 1.0 / math.sqrt(HD)
EXP2 = SCALE * math.log2(math.e)
NT = (((1,), (1,)), ((), ()))


def iota(shape, dim):
    return lax.broadcasted_iota(jnp.int32, shape, dim)


def dot(a, b):
    return jnp.dot(a, b, preferred_element_type=F32)


def dot_nt(a, b):
    return lax.dot_general(a, b, NT, preferred_element_type=F32)


def offset_of(p):
    group, half, dx = lax.div(p, 8), lax.rem(lax.div(p, 4), 2), lax.rem(p, 4)
    return NZ + half * (2 * group + 1) - group, dx


def offset_vec(p):
    group, half, dx = p >> 3, (p >> 2) & 1, p & 3
    return NZ + half * (2 * group + 1) - group, dx


def one_hots(z, x, home, shape, dim):
    n = iota(shape, dim)
    dz, dx = offset_vec(n >> 4)
    dest = (((z + dz) & (NZ - 1)) << 2) | ((x + dx) & (NX - 1))
    return [(home == dest * JB + j).astype(BF16) for j in range(JB)]


def split3(v):
    hi = v.astype(BF16)
    rest = v - hi.astype(F32)
    mid = rest.astype(BF16)
    return hi, mid, (rest - mid.astype(F32)).astype(BF16)


def kernel(
    q_ref, span_ref, cache_ref, ch_ref, home_ref, w_ref, att_ref, proj_ref,
    kbuf, vbuf, wbuf, qsend, qrecv, osend, orecv, lsend, lrecv, sp, s_scr, p_scr, ret, own_o, own_l, rs_send, rs_recv,
    lsem, wsem, q_ss, q_rs, o_ss, o_rs, l_ss, l_rs, a_ss, a_rs, b_ss, b_rs, r_ss, r_rs,
):
    me = lax.axis_index("ctx")
    kv = lax.axis_index("kvh")
    z, x = lax.div(me, NX), lax.rem(me, NX)

    def peer(p, sign=1):
        dz, dx = offset_of(p)
        if sign < 0:
            dz, dx = 2 * NZ - dz, NX - dx
        return lax.rem(z + dz, NZ) * NX + lax.rem(x + dx, NX)

    loads = []
    for j in range(JB):
        rows = pl.ds(j * BL, BL)
        loads.append(pltpu.make_async_copy(cache_ref.at[0, 0, rows], kbuf.at[j], lsem.at[2 * j]))
        loads.append(pltpu.make_async_copy(cache_ref.at[1, 0, rows], vbuf.at[j], lsem.at[2 * j + 1]))
    w_load = pltpu.make_async_copy(w_ref, wbuf, wsem)
    for load in loads:
        load.start()
    w_load.start()

    barrier = pltpu.get_barrier_semaphore()

    @pl.loop(1, N)
    def _(p):
        pl.semaphore_signal(barrier, inc=1, device_id={"ctx": peer(p)}, device_id_type=MESH)

    @pl.loop(1, NK)
    def _(i):
        pl.semaphore_signal(barrier, inc=1, device_id={"kvh": lax.rem(kv + i, NK)}, device_id_type=MESH)

    width = 4 * QD
    lanes = iota((1, 128), 1)
    c4 = []
    for t in range(TOP):
        v = ch_ref[t, :, pl.ds(pl.multiple_of(lax.div(me, 2) * 128, 128), 128)]
        mine = jnp.where((lanes >> 6) == lax.rem(me, 2), v, jnp.concatenate([v[:, QD:], v[:, :QD]], axis=1))
        c4.append(jnp.concatenate([mine, mine], axis=1))
    chosen = functools.reduce(jnp.logical_or, [iota((NB, width), 0) == c for c in c4]).astype(BF16)
    home = home_ref[...]
    nrow = PT * TILES * 16
    places = one_hots(z, x, home, (nrow, 1), 0)
    r0, r1 = iota((width, width), 0), iota((width, width), 1)
    earlier = jnp.logical_and((r0 >> 6) == (r1 >> 6), r0 < r1).astype(BF16)
    rown = iota((nrow, width), 0)
    keep_gg = ((rown >> 2) & 3) == (iota((nrow, width), 1) >> 6)
    rank_n = (rown & 3).astype(F32)
    q = q_ref[0]
    stacked = [
        jnp.concatenate([q[:, (4 * gq + gg) * HD:(4 * gq + gg + 1) * HD] for gg in range(4)], axis=0)
        for gq in range(2)
    ]
    for j in range(JB):
        here = dot(places[j], chosen)
        rank = dot(here.astype(BF16), earlier)
        pick = jnp.where(jnp.logical_and(keep_gg, rank == rank_n), here, 0.0).astype(BF16)
        for gq in range(2):
            rows = dot(pick, stacked[gq]).astype(BF16).reshape(N, 16, HD)
            qsend[:, j, gq * 16:(gq + 1) * 16, :] = rows

    sp[x, :, pl.ds(pl.multiple_of(z * QD, QD), QD), :] = span_ref[:, 0]
    qrecv[0] = qsend[0]
    pl.semaphore_wait(barrier, N - 1 + NK - 1)

    @pl.loop(1, N)
    def _(p):
        pltpu.make_async_remote_copy(
            qsend.at[p], qrecv.at[p], q_ss, q_rs.at[lax.div(p, PT)], device_id={"ctx": peer(p)}, device_id_type=MESH
        ).start()

    mine_z = sp.at[x, :, pl.ds(pl.multiple_of(z * QD, QD), QD), :]

    @pl.loop(1, NZ)
    def _(i):
        pltpu.make_async_remote_copy(
            mine_z, mine_z, a_ss, a_rs, device_id={"ctx": lax.rem(z + i, NZ) * NX + x}, device_id_type=MESH
        ).start()

    c8 = jnp.concatenate(c4 + [jnp.zeros((8 - TOP, width), jnp.int32)], axis=0).astype(F32).T
    place_n = one_hots(z, x, home, (nrow, 1), 0)
    keep_t = (iota((width, nrow), 0) >> 6) == ((iota((width, nrow), 1) >> 2) & 3)
    rank_t = (iota((width, nrow), 1) & 3).astype(F32)
    later = jnp.logical_and((r0 >> 6) == (r1 >> 6), r1 < r0).astype(BF16)
    blocks = iota((width, NB), 1).astype(F32)
    one_t = [(c8[:, t:t + 1] == blocks).astype(BF16) for t in range(TOP)]
    any_t = one_t[0] + one_t[1] + one_t[2]
    f0, f1 = iota((nrow, 128), 0), iota((nrow, 128), 1)
    first_gg = ((f0 >> 2) & 3) == 0
    by_p = jnp.logical_and(first_gg, (f0 >> 4) == f1).astype(BF16)
    pick_p = [None] * TOP
    pick_jk = [None] * TOP
    for j in range(JB):
        rank = dot(later, dot_nt(any_t, place_n[j]).astype(BF16))
        keep = jnp.logical_and(keep_t, rank == rank_t)
        to_lane = jnp.logical_and(
            jnp.logical_and(first_gg, (f1 >> 5) == j), (f0 & 3) == (f1 & 3)
        ).astype(BF16)
        for t in range(TOP):
            pick = jnp.where(keep, dot_nt(one_t[t], place_n[j]), 0.0).astype(BF16)
            for gg in range(4):
                ret[j, pl.ds((gg * TOP + t) * QD, QD), :] = pick[gg * QD:(gg + 1) * QD]
            part_p, part_jk = dot(pick[:QD], by_p), dot(pick[:QD], to_lane)
            pick_p[t] = part_p if j == 0 else pick_p[t] + part_p
            pick_jk[t] = part_jk if j == 0 else pick_jk[t] + part_jk
    pick_p = jnp.concatenate(pick_p, axis=0).astype(BF16)
    pick_jk = jnp.concatenate(pick_jk, axis=0)
    own_l[1, 0:TOP * QD, :] = pick_jk
    own_l[1, TOP * QD:2 * TOP * QD, :] = pick_p.astype(F32)

    ones = jnp.ones((BL, HD), BF16)

    def softmax_rows(slot, keys, scores_of, values):
        peak = None
        step = 512
        for c in range(keys // step):
            s = scores_of(c)
            s_scr[slot, :, c * step:(c + 1) * step] = s
            for i in range(step // 128):
                piece = s[:, i * 128:(i + 1) * 128]
                peak = piece if peak is None else jnp.maximum(peak, piece)
        peak = jnp.max(peak, axis=1, keepdims=True)
        for c in range(keys // step):
            cols = slice(c * step, (c + 1) * step)
            p_scr[slot, :, cols] = jnp.exp2((s_scr[slot, :, cols] - peak) * EXP2).astype(BF16)
        acc = dot(p_scr[slot, :, :keys], jnp.concatenate([values, ones[:keys]], axis=1))
        total = acc[:, HD:]
        return acc[:, :HD] / total, peak * SCALE + jnp.log(total)

    for load in loads:
        load.wait()

    lane_of = iota((RT, 128), 1)
    row_in = iota((RT, 128), 0) & 31

    @pl.loop(0, TILES)
    def _(tile):
        @pl.when(tile == 0)
        def _():
            part = qrecv.at[pl.ds(0, PT - 1)]
            pltpu.make_async_copy(part, part, q_rs.at[0]).wait()

        @pl.when(tile > 0)
        def _():
            part = qrecv.at[pl.ds(0, PT)]
            pltpu.make_async_copy(part, part, q_rs.at[tile]).wait()

        @pl.when(tile == 1)
        def _():
            part = sp.at[0, :, pl.ds(0, (NZ - 1) * QD), :]
            pltpu.make_async_copy(part, part, a_rs).wait()

            @pl.loop(1, NX)
            def _(i):
                pltpu.make_async_remote_copy(
                    sp.at[x], sp.at[x], b_ss, b_rs, device_id={"ctx": z * NX + lax.rem(x + i, NX)}, device_id_type=MESH
                ).start()

        base = tile * PT
        lse_rows = jnp.zeros((PT, 128), F32)
        for j in range(JB):
            rows = qrecv[pl.ds(base, PT), j].reshape(RT, HD)
            out, lse = softmax_rows(
                j, BL, lambda c: dot_nt(rows, kbuf[j, c * 512:(c + 1) * 512, :]), vbuf[j]
            )
            osend[pl.ds(base, PT), j] = out.astype(BF16).reshape(PT, 32, HD)
            lse = jnp.where(lane_of == row_in + j * 32, lse, 0.0)
            lse_rows += jnp.sum(lse.reshape(PT, 32, 128), axis=1)
        lsend[pl.ds(base, PT)] = lse_rows.reshape(PT, 1, 128)

        @pl.loop(0, PT)
        def _(i):
            p = base + i

            @pl.when(p > 0)
            def _():
                who = {"ctx": peer(p, -1)}
                pltpu.make_async_remote_copy(
                    osend.at[p], orecv.at[p], o_ss, o_rs, device_id=who, device_id_type=MESH
                ).start()
                pltpu.make_async_remote_copy(
                    lsend.at[p], lrecv.at[p], l_ss, l_rs, device_id=who, device_id_type=MESH
                ).start()

    orecv[0] = osend[0]
    lrecv[0] = lsend[0]

    part = sp.at[pl.ds(0, NX - 1)]
    pltpu.make_async_copy(part, part, b_rs).wait()
    for half in range(2):
        rows = jnp.concatenate([q_ref[0, :, (4 * half + i) * HD:(4 * half + i + 1) * HD] for i in range(4)], axis=0)
        row_pos = me * QD + (iota((RT, 512), 0) & (QD - 1))
        col = iota((RT, 512), 1)

        def own_scores(c):
            key_pos = (col >> 6) * (NX * QD) + c * QD + (col & (QD - 1))
            return jnp.where(key_pos <= row_pos, dot_nt(rows, sp[c, 0]), -1e30)

        values = jnp.concatenate([sp[c, 1] for c in range(NX)], axis=0)
        out, lse = softmax_rows(half, NX * 512, own_scores, values)
        own_o[half * RT:(half + 1) * RT, :] = out
        own_l[0, half * RT:(half + 1) * RT, :] = lse

    part = orecv.at[pl.ds(0, N - 1)]
    pltpu.make_async_copy(part, part, o_rs).wait()
    part = lrecv.at[pl.ds(0, N - 1)]
    pltpu.make_async_copy(part, part, l_rs).wait()

    pick_jk = own_l[1, 0:TOP * QD, :]
    pick_p = own_l[1, TOP * QD:2 * TOP * QD, 0:N].astype(BF16)
    pieces = jnp.concatenate(split3(lrecv[...].reshape(N, 128)), axis=1)
    picked = dot(pick_p, pieces)
    picked = jnp.concatenate([picked[:, i * 128:(i + 1) * 128] * pick_jk for i in range(3)], axis=1).astype(BF16)
    e0, e1 = iota((3 * 128, GR * HD), 0) & 127, iota((3 * 128, GR * HD), 1)
    spread = jnp.logical_and(e0 < 64, ((e0 >> 2) & 7) == (e1 >> 7)).astype(BF16)
    far_lse = dot(picked, spread)
    for gq in range(2):
        parts = sum(dot(ret[j], orecv[:, j, gq * 16:(gq + 1) * 16, :].reshape(nrow, HD)) for j in range(JB))
        for gg in range(4):
            g = gq * 4 + gg
            lses = [own_l[0, g * QD:(g + 1) * QD, :]]
            outs = [own_o[g * QD:(g + 1) * QD, :]]
            for t in range(TOP):
                lses.append(far_lse[t * QD:(t + 1) * QD, g * HD:(g + 1) * HD])
                outs.append(parts[(gg * TOP + t) * QD:(gg * TOP + t + 1) * QD])
            peak = functools.reduce(jnp.maximum, lses)
            factors = [jnp.exp(v - peak) for v in lses]
            mixed = sum(f * o for f, o in zip(factors, outs)) / sum(factors)
            att_ref[0, :, g * HD:(g + 1) * HD] = mixed.astype(BF16)

    w_load.wait()
    att = att_ref[0]
    half = COLS // 2
    step = 512
    for c in range(half // step):
        left = dot(att, wbuf[:, c * step:(c + 1) * step])
        right = dot(att, wbuf[:, half + c * step:half + (c + 1) * step])
        for k in range(NK):
            both = jnp.concatenate([left[k * 8:(k + 1) * 8], right[k * 8:(k + 1) * 8]], axis=0)
            rs_send[k, :, c * step:(c + 1) * step] = both.astype(BF16)

    @pl.loop(1, NK)
    def _(i):
        dst = lax.rem(kv + i, NK)
        pltpu.make_async_remote_copy(
            rs_send.at[dst], rs_recv.at[i], r_ss, r_rs, device_id={"kvh": dst}, device_id_type=MESH
        ).start()

    part = rs_recv.at[pl.ds(0, NK - 1)]
    pltpu.make_async_copy(part, part, r_rs).wait()
    total = rs_send[kv].astype(F32)
    for i in range(1, NK):
        total += rs_recv[i].astype(F32)
    proj_ref[:, :half] = total[:8].astype(BF16)
    proj_ref[:, half:] = total[8:].astype(BF16)

    for buf, sem in ((qsend, q_ss), (osend, o_ss), (lsend, l_ss)):
        part = buf.at[pl.ds(0, N - 1)]
        pltpu.make_async_copy(part, part, sem).wait()
    part = sp.at[0, :, pl.ds(0, (NZ - 1) * QD), :]
    pltpu.make_async_copy(part, part, a_ss).wait()
    part = sp.at[pl.ds(0, NX - 1)]
    pltpu.make_async_copy(part, part, b_ss).wait()
    part = rs_send.at[pl.ds(0, NK - 1)]
    pltpu.make_async_copy(part, part, r_ss).wait()


def on_device(queries, span_kv, cache_kv, choices, block_home, out_weight):
    vmem = pl.BlockSpec(memory_space=pltpu.VMEM)
    hbm = pl.BlockSpec(memory_space=pl.ANY)
    dma = pltpu.SemaphoreType.DMA
    attended, projected = pl.pallas_call(
        kernel,
        out_shape=(
            jax.ShapeDtypeStruct((1, QD, GR * HD), BF16),
            jax.ShapeDtypeStruct((8, COLS), BF16),
        ),
        in_specs=[vmem, vmem, hbm, vmem, vmem, hbm],
        out_specs=(vmem, vmem),
        scratch_shapes=[
            pltpu.VMEM((JB, BL, HD), BF16),
            pltpu.VMEM((JB, BL, HD), BF16),
            pltpu.VMEM((GR * HD, COLS), BF16),
            pltpu.VMEM((N, JB, 32, HD), BF16),
            pltpu.VMEM((N, JB, 32, HD), BF16),
            pltpu.VMEM((N, JB, 32, HD), BF16),
            pltpu.VMEM((N, JB, 32, HD), BF16),
            pltpu.VMEM((N, 1, 128), F32),
            pltpu.VMEM((N, 1, 128), F32),
            pltpu.VMEM((NX, 2, NZ * QD, HD), BF16),
            pltpu.VMEM((JB, RT, BL), F32),
            pltpu.VMEM((JB, RT, BL), BF16),
            pltpu.VMEM((JB, 4 * TOP * QD, N * 16), BF16),
            pltpu.VMEM((GR * QD, HD), F32),
            pltpu.VMEM((2, GR * QD, HD), F32),
            pltpu.VMEM((NK, 16, COLS // 2), BF16),
            pltpu.VMEM((NK, 16, COLS // 2), BF16),
            dma((4,)),
            dma,
            dma,
            dma((TILES,)),
            dma, dma, dma, dma, dma, dma, dma, dma, dma, dma,
        ],
        compiler_params=pltpu.CompilerParams(
            collective_id=0, has_side_effects=True, vmem_limit_bytes=56 * 2**20
        ),
    )(
        queries,
        span_kv,
        cache_kv,
        jnp.transpose(choices, (2, 0, 1)),
        block_home.reshape(1, NB),
        out_weight,
    )
    return attended, projected


def solution(mesh):
    return jax.shard_map(
        on_device,
        mesh=mesh,
        in_specs=(
            P("kvh", "ctx", None),
            P(None, "kvh", "ctx", None),
            P(None, "kvh", "ctx", None),
            P("kvh", None, None),
            P(),
            P("kvh", None),
        ),
        out_specs=(P("kvh", "ctx", None), P(("ctx", "kvh"), None)),
        check_vma=False,
    )
```

```python
import functools
import math

import jax
import jax.numpy as jnp
from jax import lax
from jax.experimental import pallas as pl
from jax.experimental.pallas import tpu as pltpu
from jax.sharding import PartitionSpec as P

MESH = pl.DeviceIdType.MESH
F32 = jnp.float32
BF16 = jnp.bfloat16

NZ, NX, NY = 8, 4, 4
N = NZ * NX
QD = 64
HD = 128
GR = 8
TOP = 3
MOST = 4
NB = 64
BL = 4096
JB = 2
COLS = 4096
CHUNKS = 4
CW = COLS // CHUNKS
TILES = 4
PT = N // TILES
RT = PT * GR * MOST
SCALE = 1.0 / math.sqrt(HD)
EXP2 = SCALE * math.log2(math.e)
NT = (((1,), (1,)), ((), ()))


def iota(shape, dim):
    return lax.broadcasted_iota(jnp.int32, shape, dim)


def dot(a, b):
    return jnp.dot(a, b, preferred_element_type=F32)


def dot_nt(a, b):
    return lax.dot_general(a, b, NT, preferred_element_type=F32)


def offset_of(p):
    dx, i = lax.div(p, NZ), lax.rem(p, NZ)
    return NZ + (2 * lax.rem(i, 2) - 1) * lax.div(i + 1, 2), dx


def offset_vec(p):
    dx, i = p >> 3, p & 7
    return NZ + (2 * (i & 1) - 1) * ((i + 1) >> 1), dx


def one_hots(z, x, home, shape, dim):
    n = iota(shape, dim)
    dz, dx = offset_vec(n >> 4)
    dest = (((z + dz) & (NZ - 1)) << 2) | ((x + dx) & (NX - 1))
    return [(home == dest * JB + j).astype(BF16) for j in range(JB)]


def send(src, dst, ss, rs, who):
    pltpu.make_async_remote_copy(src, dst, ss, rs, device_id=who, device_id_type=MESH).start()


def wait_for(part, sem):
    pltpu.make_async_copy(part, part, sem).wait()


def split3(v):
    hi = v.astype(BF16)
    rest = v - hi.astype(F32)
    mid = rest.astype(BF16)
    return hi, mid, (rest - mid.astype(F32)).astype(BF16)


def kernel(
    q_hbm, span_ref, cache_ref, ch_hbm, home_hbm, w_ref, att_ref, proj_ref,
    q_ref, ch_ref, home_ref, kbuf, vbuf, wbuf, qsend, qrecv, osend, orecv, lsend, lrecv, sp, s_scr, p_scr, ret, own_o, own_l, r_stage, r_recv, y_send, y_recv,
    isem, lsem, wsem, q_ss, q_rs, o_ss, o_rs, l_ss, l_rs, a_ss, a_rs, b_ss, b_rs, r_ss, r_rs, y_ss, y_rs,
):
    me = lax.axis_index("ctx")
    kv = lax.axis_index("kvh")
    z, x = lax.div(me, NX), lax.rem(me, NX)

    def peer(p, sign=1):
        dz, dx = offset_of(p)
        if sign < 0:
            dz, dx = 2 * NZ - dz, NX - dx
        return lax.rem(z + dz, NZ) * NX + lax.rem(x + dx, NX)

    mine_z = sp.at[x, :, pl.ds(pl.multiple_of(z * QD, QD), QD), :]
    pair = pl.ds(pl.multiple_of(lax.div(me, 2) * 128, 128), 128)
    inputs = [
        pltpu.make_async_copy(span_ref.at[:, 0], mine_z, isem.at[0]),
        pltpu.make_async_copy(ch_hbm.at[:, :, pair], ch_ref, isem.at[1]),
        pltpu.make_async_copy(home_hbm, home_ref, isem.at[2]),
        pltpu.make_async_copy(q_hbm, q_ref, isem.at[3]),
    ]
    for load in inputs:
        load.start()
    loads = []
    for j in range(JB):
        rows = pl.ds(j * BL, BL)
        loads.append(pltpu.make_async_copy(cache_ref.at[0, 0, rows], kbuf.at[j], lsem.at[2 * j]))
        loads.append(pltpu.make_async_copy(cache_ref.at[1, 0, rows], vbuf.at[j], lsem.at[2 * j + 1]))
    w_load = pltpu.make_async_copy(w_ref, wbuf, wsem)
    for load in loads:
        load.start()
    w_load.start()

    barrier = pltpu.get_barrier_semaphore()

    @pl.loop(1, N)
    def _(p):
        pl.semaphore_signal(barrier, inc=1, device_id={"ctx": peer(p)}, device_id_type=MESH)

    core, y = lax.rem(kv, 2), lax.div(kv, 2)
    sibling = {"kvh": kv + 1 - 2 * core}

    def along_y(i):
        return lax.rem(y + i, NY)

    pl.semaphore_signal(barrier, inc=1, device_id=sibling, device_id_type=MESH)

    @pl.loop(1, NY)
    def _(i):
        pl.semaphore_signal(barrier, inc=1, device_id={"kvh": 2 * along_y(i) + core}, device_id_type=MESH)

    inputs[0].wait()
    pl.semaphore_wait(barrier, N - 1 + 1 + NY - 1)

    @pl.loop(1, NZ)
    def _(i):
        send(mine_z, mine_z, a_ss, a_rs, {"ctx": lax.rem(z + i, NZ) * NX + x})

    for load in inputs[1:]:
        load.wait()
    width = 4 * QD
    lanes = iota((1, 128), 1)
    c4 = []
    for t in range(TOP):
        v = ch_ref[t]
        mine = jnp.where((lanes >> 6) == lax.rem(me, 2), v, jnp.concatenate([v[:, QD:], v[:, :QD]], axis=1))
        c4.append(jnp.concatenate([mine, mine], axis=1))
    chosen = functools.reduce(jnp.logical_or, [iota((NB, width), 0) == c for c in c4]).astype(BF16)
    home = home_ref[...]
    nrow = PT * TILES * 16
    places = one_hots(z, x, home, (nrow, 1), 0)
    r0, r1 = iota((width, width), 0), iota((width, width), 1)
    earlier = jnp.logical_and((r0 >> 6) == (r1 >> 6), r0 < r1).astype(BF16)
    rown = iota((nrow, width), 0)
    keep_gg = ((rown >> 2) & 3) == (iota((nrow, width), 1) >> 6)
    rank_n = (rown & 3).astype(F32)
    q = q_ref[0]
    stacked = [
        jnp.concatenate([q[:, (4 * gq + gg) * HD:(4 * gq + gg + 1) * HD] for gg in range(4)], axis=0)
        for gq in range(2)
    ]
    for j in range(JB):
        here = dot(places[j], chosen)
        rank = dot(here.astype(BF16), earlier)
        pick = jnp.where(jnp.logical_and(keep_gg, rank == rank_n), here, 0.0).astype(BF16)
        for gq in range(2):
            rows = dot(pick, stacked[gq]).astype(BF16).reshape(N, 16, HD)
            qsend[:, j, gq * 16:(gq + 1) * 16, :] = rows

    qrecv[0] = qsend[0]

    @pl.loop(1, N)
    def _(p):
        send(qsend.at[p], qrecv.at[p], q_ss, q_rs.at[lax.div(p, PT)], {"ctx": peer(p)})

    c8 = jnp.concatenate(c4 + [jnp.zeros((8 - TOP, width), jnp.int32)], axis=0).astype(F32).T
    place_n = one_hots(z, x, home, (nrow, 1), 0)
    keep_t = (iota((width, nrow), 0) >> 6) == ((iota((width, nrow), 1) >> 2) & 3)
    rank_t = (iota((width, nrow), 1) & 3).astype(F32)
    later = jnp.logical_and((r0 >> 6) == (r1 >> 6), r1 < r0).astype(BF16)
    blocks = iota((width, NB), 1).astype(F32)
    one_t = [(c8[:, t:t + 1] == blocks).astype(BF16) for t in range(TOP)]
    any_t = one_t[0] + one_t[1] + one_t[2]
    f0, f1 = iota((nrow, 128), 0), iota((nrow, 128), 1)
    first_gg = ((f0 >> 2) & 3) == 0
    by_p = jnp.logical_and(first_gg, (f0 >> 4) == f1).astype(BF16)
    pick_p = [None] * TOP
    pick_jk = [None] * TOP
    for j in range(JB):
        rank = dot(later, dot_nt(any_t, place_n[j]).astype(BF16))
        keep = jnp.logical_and(keep_t, rank == rank_t)
        to_lane = jnp.logical_and(
            jnp.logical_and(first_gg, (f1 >> 5) == j), (f0 & 3) == (f1 & 3)
        ).astype(BF16)
        for t in range(TOP):
            pick = jnp.where(keep, dot_nt(one_t[t], place_n[j]), 0.0).astype(BF16)
            for gg in range(4):
                ret[j, pl.ds((gg * TOP + t) * QD, QD), :] = pick[gg * QD:(gg + 1) * QD]
            part_p, part_jk = dot(pick[:QD], by_p), dot(pick[:QD], to_lane)
            pick_p[t] = part_p if j == 0 else pick_p[t] + part_p
            pick_jk[t] = part_jk if j == 0 else pick_jk[t] + part_jk
    pick_p = jnp.concatenate(pick_p, axis=0).astype(BF16)
    pick_jk = jnp.concatenate(pick_jk, axis=0)
    own_l[1, 0:TOP * QD, :] = pick_jk
    own_l[1, TOP * QD:2 * TOP * QD, :] = pick_p.astype(F32)

    ones = jnp.ones((BL, HD), BF16)

    def softmax_rows(slot, keys, scores_of, values):
        peak = None
        step = 512
        for c in range(keys // step):
            s = scores_of(c)
            s_scr[slot, :, c * step:(c + 1) * step] = s
            for i in range(step // 128):
                piece = s[:, i * 128:(i + 1) * 128]
                peak = piece if peak is None else jnp.maximum(peak, piece)
        peak = jnp.max(peak, axis=1, keepdims=True)
        for c in range(keys // step):
            cols = slice(c * step, (c + 1) * step)
            p_scr[slot, :, cols] = jnp.exp2((s_scr[slot, :, cols] - peak) * EXP2).astype(BF16)
        acc = dot(p_scr[slot, :, :keys], jnp.concatenate([values, ones[:keys]], axis=1))
        total = acc[:, HD:]
        return acc[:, :HD] / total, peak * SCALE + jnp.log(total)

    for load in loads:
        load.wait()

    part = sp.at[0, :, pl.ds(0, (NZ - 1) * QD), :]
    wait_for(part, a_rs)

    @pl.loop(1, NX)
    def _(i):
        send(sp.at[x], sp.at[x], b_ss, b_rs, {"ctx": z * NX + lax.rem(x + i, NX)})

    lane_of = iota((RT, 128), 1)
    row_in = iota((RT, 128), 0) & 31

    @pl.loop(0, TILES)
    def _(tile):
        @pl.when(tile == 0)
        def _():
            part = qrecv.at[pl.ds(0, PT - 1)]
            wait_for(part, q_rs.at[0])

        @pl.when(tile > 0)
        def _():
            part = qrecv.at[pl.ds(0, PT)]
            wait_for(part, q_rs.at[tile])

        base = tile * PT
        lse_rows = jnp.zeros((PT, 128), F32)
        for j in range(JB):
            rows = qrecv[pl.ds(base, PT), j].reshape(RT, HD)
            out, lse = softmax_rows(
                j, BL, lambda c: dot_nt(rows, kbuf[j, c * 512:(c + 1) * 512, :]), vbuf[j]
            )
            osend[pl.ds(base, PT), j] = out.astype(BF16).reshape(PT, 32, HD)
            lse = jnp.where(lane_of == row_in + j * 32, lse, 0.0)
            lse_rows += jnp.sum(lse.reshape(PT, 32, 128), axis=1)
        lsend[pl.ds(base, PT)] = lse_rows.reshape(PT, 1, 128)

        @pl.loop(0, PT)
        def _(i):
            p = base + i

            @pl.when(p > 0)
            def _():
                who = {"ctx": peer(p, -1)}
                send(osend.at[p], orecv.at[p], o_ss, o_rs, who)
                send(lsend.at[p], lrecv.at[p], l_ss, l_rs, who)

    orecv[0] = osend[0]
    lrecv[0] = lsend[0]

    part = sp.at[pl.ds(0, NX - 1)]
    wait_for(part, b_rs)
    for half in range(2):
        rows = jnp.concatenate([q_ref[0, :, (4 * half + i) * HD:(4 * half + i + 1) * HD] for i in range(4)], axis=0)
        row_pos = me * QD + (iota((RT, 512), 0) & (QD - 1))
        col = iota((RT, 512), 1)

        def own_scores(c):
            key_pos = (col >> 6) * (NX * QD) + c * QD + (col & (QD - 1))
            return jnp.where(key_pos <= row_pos, dot_nt(rows, sp[c, 0]), -1e30)

        values = jnp.concatenate([sp[c, 1] for c in range(NX)], axis=0)
        out, lse = softmax_rows(half, NX * 512, own_scores, values)
        own_o[half * RT:(half + 1) * RT, :] = out
        own_l[0, half * RT:(half + 1) * RT, :] = lse

    part = orecv.at[pl.ds(0, N - 1)]
    wait_for(part, o_rs)
    part = lrecv.at[pl.ds(0, N - 1)]
    wait_for(part, l_rs)

    pick_jk = own_l[1, 0:TOP * QD, :]
    pick_p = own_l[1, TOP * QD:2 * TOP * QD, 0:N].astype(BF16)
    pieces = jnp.concatenate(split3(lrecv[...].reshape(N, 128)), axis=1)
    picked = dot(pick_p, pieces)
    picked = jnp.concatenate([picked[:, i * 128:(i + 1) * 128] * pick_jk for i in range(3)], axis=1).astype(BF16)
    e0, e1 = iota((3 * 128, GR * HD), 0) & 127, iota((3 * 128, GR * HD), 1)
    spread = jnp.logical_and(e0 < 64, ((e0 >> 2) & 7) == (e1 >> 7)).astype(BF16)
    far_lse = dot(picked, spread)
    for gq in range(2):
        parts = sum(dot(ret[j], orecv[:, j, gq * 16:(gq + 1) * 16, :].reshape(nrow, HD)) for j in range(JB))
        for gg in range(4):
            g = gq * 4 + gg
            lses = [own_l[0, g * QD:(g + 1) * QD, :]]
            outs = [own_o[g * QD:(g + 1) * QD, :]]
            for t in range(TOP):
                lses.append(far_lse[t * QD:(t + 1) * QD, g * HD:(g + 1) * HD])
                outs.append(parts[(gg * TOP + t) * QD:(gg * TOP + t + 1) * QD])
            peak = functools.reduce(jnp.maximum, lses)
            factors = [jnp.exp(v - peak) for v in lses]
            mixed = sum(f * o for f, o in zip(factors, outs)) / sum(factors)
            att_ref[0, :, g * HD:(g + 1) * HD] = mixed.astype(BF16)

    w_load.wait()
    att = att_ref[0]

    def over_y(c):
        wait_for(r_recv.at[c], r_rs.at[c])
        both = r_stage[core, c].astype(F32) + r_recv[c].astype(F32)
        y_send[c] = both.astype(BF16)

        @pl.loop(1, NY)
        def _(i):
            to = along_y(i)
            send(y_send.at[c, to], y_recv.at[c, i], y_ss, y_rs.at[c], {"kvh": 2 * to + core})

    for c in range(CHUNKS):
        part = dot(att, wbuf[:, c * CW:(c + 1) * CW])
        for k in range(2 * NY):
            rows = part[k * 8:(k + 1) * 8]
            both = jnp.concatenate([rows[:, :CW // 2], rows[:, CW // 2:]], axis=0)
            r_stage[k % 2, c, k // 2] = both.astype(BF16)
        send(r_stage.at[1 - core, c], r_recv.at[c], r_ss, r_rs.at[c], sibling)
        if c > 0:
            over_y(c - 1)
    over_y(CHUNKS - 1)
    for c in range(CHUNKS):
        wait_for(y_recv.at[c, pl.ds(1, NY - 1)], y_rs.at[c])
        total = y_send[c, y].astype(F32)
        for i in range(1, NY):
            total += y_recv[c, i].astype(F32)
        proj_ref[:, c * CW:c * CW + CW // 2] = total[:8].astype(BF16)
        proj_ref[:, c * CW + CW // 2:(c + 1) * CW] = total[8:].astype(BF16)

    for buf, sem in ((qsend, q_ss), (osend, o_ss), (lsend, l_ss)):
        part = buf.at[pl.ds(0, N - 1)]
        wait_for(part, sem)
    part = sp.at[0, :, pl.ds(0, (NZ - 1) * QD), :]
    wait_for(part, a_ss)
    part = sp.at[pl.ds(0, NX - 1)]
    wait_for(part, b_ss)
    wait_for(r_recv, r_ss)
    wait_for(y_recv.at[:, pl.ds(1, NY - 1)], y_ss)


def on_device(queries, span_kv, cache_kv, choices, block_home, out_weight):
    vmem = pl.BlockSpec(memory_space=pltpu.VMEM)
    hbm = pl.BlockSpec(memory_space=pl.ANY)
    dma = pltpu.SemaphoreType.DMA
    attended, projected = pl.pallas_call(
        kernel,
        out_shape=(
            pltpu.VMEM((1, QD, GR * HD), BF16),
            pltpu.VMEM((8, COLS), BF16),
        ),
        in_specs=[hbm] * 6,
        out_specs=(vmem, vmem),
        scratch_shapes=[
            pltpu.VMEM((1, QD, GR * HD), BF16),
            pltpu.VMEM((TOP, 1, 128), jnp.int32),
            pltpu.VMEM((1, NB), jnp.int32),
            pltpu.VMEM((JB, BL, HD), BF16),
            pltpu.VMEM((JB, BL, HD), BF16),
            pltpu.VMEM((GR * HD, COLS), BF16),
            pltpu.VMEM((N, JB, 32, HD), BF16),
            pltpu.VMEM((N, JB, 32, HD), BF16),
            pltpu.VMEM((N, JB, 32, HD), BF16),
            pltpu.VMEM((N, JB, 32, HD), BF16),
            pltpu.VMEM((N, 1, 128), F32),
            pltpu.VMEM((N, 1, 128), F32),
            pltpu.VMEM((NX, 2, NZ * QD, HD), BF16),
            pltpu.VMEM((JB, RT, BL), F32),
            pltpu.VMEM((JB, RT, BL), BF16),
            pltpu.VMEM((JB, 4 * TOP * QD, N * 16), BF16),
            pltpu.VMEM((GR * QD, HD), F32),
            pltpu.VMEM((2, GR * QD, HD), F32),
            pltpu.VMEM((2, CHUNKS, NY, 16, CW // 2), BF16),
            pltpu.VMEM((CHUNKS, NY, 16, CW // 2), BF16),
            pltpu.VMEM((CHUNKS, NY, 16, CW // 2), BF16),
            pltpu.VMEM((CHUNKS, NY, 16, CW // 2), BF16),
            dma((4,)),
            dma((4,)),
            dma,
            dma,
            dma((TILES,)),
            dma, dma, dma, dma, dma, dma, dma, dma,
            dma,
            dma((CHUNKS,)),
            dma,
            dma((CHUNKS,)),
        ],
        compiler_params=pltpu.CompilerParams(
            collective_id=0, has_side_effects=True, vmem_limit_bytes=56 * 2**20
        ),
    )(
        queries,
        span_kv,
        cache_kv,
        jnp.transpose(choices, (2, 0, 1)),
        block_home.reshape(1, NB),
        out_weight,
    )
    return attended, projected


def solution(mesh):
    return jax.shard_map(
        on_device,
        mesh=mesh,
        in_specs=(
            P("kvh", "ctx", None),
            P(None, "kvh", "ctx", None),
            P(None, "kvh", "ctx", None),
            P("kvh", None, None),
            P(),
            P("kvh", None),
        ),
        out_specs=(P("kvh", "ctx", None), P(("ctx", "kvh"), None)),
        check_vma=False,
    )
```

```python
import functools
import math

import jax
import jax.numpy as jnp
from jax import lax
from jax.experimental import pallas as pl
from jax.experimental.pallas import tpu as pltpu
from jax.sharding import PartitionSpec as P

MESH = pl.DeviceIdType.MESH
F32 = jnp.float32
BF16 = jnp.bfloat16

NZ, NX, NY = 8, 4, 4
N = NZ * NX
QD = 64
HD = 128
GR = 8
TOP = 3
MOST = 4
NB = 64
BL = 4096
JB = 2
COLS = 4096
CHUNKS = 4
CW = COLS // CHUNKS
TILES = 4
PT = N // TILES
RT = PT * GR * MOST
SCALE = 1.0 / math.sqrt(HD)
EXP2 = SCALE * math.log2(math.e)
NT = (((1,), (1,)), ((), ()))


def iota(shape, dim):
    return lax.broadcasted_iota(jnp.int32, shape, dim)


def dot(a, b):
    return jnp.dot(a, b, preferred_element_type=F32)


def dot_nt(a, b):
    return lax.dot_general(a, b, NT, preferred_element_type=F32)


def offset_of(p):
    dx, i = lax.div(p, NZ), lax.rem(p, NZ)
    return NZ + (2 * lax.rem(i, 2) - 1) * lax.div(i + 1, 2), dx


def offset_vec(p):
    dx, i = p >> 3, p & 7
    return NZ + (2 * (i & 1) - 1) * ((i + 1) >> 1), dx


def one_hots(z, x, home, shape, dim):
    n = iota(shape, dim)
    dz, dx = offset_vec(n >> 4)
    dest = (((z + dz) & (NZ - 1)) << 2) | ((x + dx) & (NX - 1))
    return [(home == dest * JB + j).astype(BF16) for j in range(JB)]


def send(src, dst, ss, rs, who):
    pltpu.make_async_remote_copy(src, dst, ss, rs, device_id=who, device_id_type=MESH).start()


def wait_for(part, sem):
    pltpu.make_async_copy(part, part, sem).wait()


def split3(v):
    hi = v.astype(BF16)
    rest = v - hi.astype(F32)
    mid = rest.astype(BF16)
    return hi, mid, (rest - mid.astype(F32)).astype(BF16)


def kernel(
    q_hbm, span_ref, cache_ref, ch_hbm, home_hbm, w_ref, att_ref, proj_ref,
    q_ref, ch_ref, home_ref, kbuf, vbuf, wbuf, qsend, qrecv, osend, orecv, lsend, lrecv, sp, s_scr, p_scr, ret, own_o, own_l, weight, r_stage, r_recv, y_send, y_recv,
    isem, lsem, wsem, q_ss, q_rs, o_ss, o_rs, l_ss, l_rs, a_ss, a_rs, a2_rs, b_ss, b_rs, r_ss, r_rs, y_ss, y_rs,
):
    me = lax.axis_index("ctx")
    kv = lax.axis_index("kvh")
    z, x = lax.div(me, NX), lax.rem(me, NX)

    def peer(p, sign=1):
        dz, dx = offset_of(p)
        if sign < 0:
            dz, dx = 2 * NZ - dz, NX - dx
        return lax.rem(z + dz, NZ) * NX + lax.rem(x + dx, NX)

    barrier = pltpu.get_barrier_semaphore()

    @pl.loop(1, N)
    def _(p):
        pl.semaphore_signal(barrier, inc=1, device_id={"ctx": peer(p)}, device_id_type=MESH)

    core, y = lax.rem(kv, 2), lax.div(kv, 2)
    sibling = {"kvh": kv + 1 - 2 * core}

    def along_y(i):
        return lax.rem(y + i, NY)

    pl.semaphore_signal(barrier, inc=1, device_id=sibling, device_id_type=MESH)

    @pl.loop(1, NY)
    def _(i):
        pl.semaphore_signal(barrier, inc=1, device_id={"kvh": 2 * along_y(i) + core}, device_id_type=MESH)

    mine_z = sp.at[x, :, pl.ds(pl.multiple_of(z * QD, QD), QD), :]
    pair = pl.ds(pl.multiple_of(lax.div(me, 2) * 128, 128), 128)
    inputs = [
        pltpu.make_async_copy(span_ref.at[:, 0], mine_z, isem.at[0]),
        pltpu.make_async_copy(ch_hbm.at[:, :, pair], ch_ref, isem.at[1]),
        pltpu.make_async_copy(home_hbm, home_ref, isem.at[2]),
        pltpu.make_async_copy(q_hbm, q_ref, isem.at[3]),
    ]
    for load in inputs:
        load.start()
    loads = []
    for j in range(JB):
        rows = pl.ds(j * BL, BL)
        loads.append(pltpu.make_async_copy(cache_ref.at[0, 0, rows], kbuf.at[j], lsem.at[2 * j]))
        loads.append(pltpu.make_async_copy(cache_ref.at[1, 0, rows], vbuf.at[j], lsem.at[2 * j + 1]))
    w_load = pltpu.make_async_copy(w_ref, wbuf, wsem)
    for load in loads:
        load.start()
    w_load.start()

    inputs[0].wait()
    pl.semaphore_wait(barrier, N - 1 + 1 + NY - 1)

    def at_z(d):
        return lax.rem(z + NZ + d, NZ)

    def send_z(src, sem, d):
        send(src, src, a_ss, sem, {"ctx": at_z(d) * NX + x})

    for d in (1, -1, 2, -2):
        send_z(mine_z, a_rs, d)

    for load in inputs[1:]:
        load.wait()
    width = 4 * QD
    lanes = iota((1, 128), 1)
    c4 = []
    for t in range(TOP):
        v = ch_ref[t]
        mine = jnp.where((lanes >> 6) == lax.rem(me, 2), v, jnp.concatenate([v[:, QD:], v[:, :QD]], axis=1))
        c4.append(jnp.concatenate([mine, mine], axis=1))
    chosen = functools.reduce(jnp.logical_or, [iota((NB, width), 0) == c for c in c4]).astype(BF16)
    home = home_ref[...]
    nrow = PT * TILES * 16
    places = one_hots(z, x, home, (nrow, 1), 0)
    r0, r1 = iota((width, width), 0), iota((width, width), 1)
    earlier = jnp.logical_and((r0 >> 6) == (r1 >> 6), r0 < r1).astype(BF16)
    rown = iota((nrow, width), 0)
    keep_gg = ((rown >> 2) & 3) == (iota((nrow, width), 1) >> 6)
    rank_n = (rown & 3).astype(F32)
    q = q_ref[0]
    stacked = [
        jnp.concatenate([q[:, (4 * gq + gg) * HD:(4 * gq + gg + 1) * HD] for gg in range(4)], axis=0)
        for gq in range(2)
    ]
    for j in range(JB):
        here = dot(places[j], chosen)
        rank = dot(here.astype(BF16), earlier)
        pick = jnp.where(jnp.logical_and(keep_gg, rank == rank_n), here, 0.0).astype(BF16)
        for gq in range(2):
            rows = dot(pick, stacked[gq]).astype(BF16).reshape(N, 16, HD)
            qsend[:, j, gq * 16:(gq + 1) * 16, :] = rows

    qrecv[0] = qsend[0]

    def send_rows(p):
        send(qsend.at[p], qrecv.at[p], q_ss, q_rs.at[lax.div(p, PT)], {"ctx": peer(p)})

    pl.loop(1, PT)(send_rows)

    wait_for(sp.at[0, :, pl.ds(0, 4 * QD), :], a_rs)
    below = pl.ds(pl.multiple_of(at_z(-2) * QD, QD), QD)
    above = pl.ds(pl.multiple_of(at_z(2) * QD, QD), QD)
    send_z(sp.at[x, :, below], a2_rs, 1)
    send_z(sp.at[x, :, above], a2_rs, -1)
    send_z(sp.at[x, 0, below], a2_rs, 2)
    send_z(sp.at[x, 1, above], a2_rs, -2)

    pl.loop(PT, N)(send_rows)

    c8 = jnp.concatenate(c4 + [jnp.zeros((8 - TOP, width), jnp.int32)], axis=0).astype(F32).T
    place_n = one_hots(z, x, home, (nrow, 1), 0)
    keep_t = (iota((width, nrow), 0) >> 6) == ((iota((width, nrow), 1) >> 2) & 3)
    rank_t = (iota((width, nrow), 1) & 3).astype(F32)
    later = jnp.logical_and((r0 >> 6) == (r1 >> 6), r1 < r0).astype(BF16)
    blocks = iota((width, NB), 1).astype(F32)
    one_t = [(c8[:, t:t + 1] == blocks).astype(BF16) for t in range(TOP)]
    any_t = one_t[0] + one_t[1] + one_t[2]
    f0, f1 = iota((nrow, 128), 0), iota((nrow, 128), 1)
    first_gg = ((f0 >> 2) & 3) == 0
    by_p = jnp.logical_and(first_gg, (f0 >> 4) == f1).astype(BF16)
    pick_p = [None] * TOP
    pick_jk = [None] * TOP
    for j in range(JB):
        rank = dot(later, dot_nt(any_t, place_n[j]).astype(BF16))
        keep = jnp.logical_and(keep_t, rank == rank_t)
        to_lane = jnp.logical_and(
            jnp.logical_and(first_gg, (f1 >> 5) == j), (f0 & 3) == (f1 & 3)
        ).astype(BF16)
        for t in range(TOP):
            pick = jnp.where(keep, dot_nt(one_t[t], place_n[j]), 0.0).astype(BF16)
            for gg in range(4):
                ret[j, pl.ds((gg * TOP + t) * QD, QD), :] = pick[gg * QD:(gg + 1) * QD]
            part_p, part_jk = dot(pick[:QD], by_p), dot(pick[:QD], to_lane)
            pick_p[t] = part_p if j == 0 else pick_p[t] + part_p
            pick_jk[t] = part_jk if j == 0 else pick_jk[t] + part_jk
    pick_p = jnp.concatenate(pick_p, axis=0).astype(BF16)
    pick_jk = jnp.concatenate(pick_jk, axis=0)
    own_l[1, 0:TOP * QD, :] = pick_jk
    own_l[1, TOP * QD:2 * TOP * QD, :] = pick_p.astype(F32)

    ones = jnp.ones((BL, HD), BF16)

    def softmax_rows(slot, keys, scores_of, values):
        peak = None
        step = 512
        for c in range(keys // step):
            s = scores_of(c)
            s_scr[slot, :, c * step:(c + 1) * step] = s
            for i in range(step // 128):
                piece = s[:, i * 128:(i + 1) * 128]
                peak = piece if peak is None else jnp.maximum(peak, piece)
        peak = jnp.max(peak, axis=1, keepdims=True)
        for c in range(keys // step):
            cols = slice(c * step, (c + 1) * step)
            p_scr[slot, :, cols] = jnp.exp2((s_scr[slot, :, cols] - peak) * EXP2).astype(BF16)
        acc = dot(p_scr[slot, :, :keys], jnp.concatenate([values, ones[:keys]], axis=1))
        total = acc[:, HD:]
        return acc[:, :HD] / total, peak * SCALE + jnp.log(total)

    for load in loads:
        load.wait()

    wait_for(sp.at[0, :, pl.ds(0, 3 * QD), :], a2_rs)

    @pl.loop(1, NX)
    def _(i):
        send(sp.at[x], sp.at[x], b_ss, b_rs, {"ctx": z * NX + lax.rem(x + i, NX)})

    lane_of = iota((RT, 128), 1)
    row_in = iota((RT, 128), 0) & 31

    @pl.loop(0, TILES)
    def _(tile):
        @pl.when(tile == 0)
        def _():
            part = qrecv.at[pl.ds(0, PT - 1)]
            wait_for(part, q_rs.at[0])

        @pl.when(tile > 0)
        def _():
            part = qrecv.at[pl.ds(0, PT)]
            wait_for(part, q_rs.at[tile])

        base = tile * PT
        lse_rows = jnp.zeros((PT, 128), F32)
        step = 512
        rows = [qrecv[pl.ds(base, PT), j].reshape(RT, HD) for j in range(JB)]

        def scores(j, c, peak):
            s = dot_nt(rows[j], kbuf[j, c * step:(c + 1) * step, :])
            s_scr[j, :, c * step:(c + 1) * step] = s
            for i in range(step // 128):
                piece = s[:, i * 128:(i + 1) * 128]
                peak = piece if peak is None else jnp.maximum(peak, piece)
            return peak

        def weigh(j, c, peak, acc):
            cols = slice(c * step, (c + 1) * step)
            p = jnp.exp2((s_scr[j, :, cols] - peak) * EXP2).astype(BF16)
            new = dot(p, jnp.concatenate([vbuf[j, cols], ones[cols]], axis=1))
            return new if acc is None else acc + new

        def finish(j, peak, acc):
            total = acc[:, HD:]
            osend[pl.ds(base, PT), j] = (acc[:, :HD] / total).astype(BF16).reshape(PT, 32, HD)
            lse = jnp.where(lane_of == row_in + j * 32, peak * SCALE + jnp.log(total), 0.0)
            return jnp.sum(lse.reshape(PT, 32, 128), axis=1)

        peak0 = peak1 = acc0 = acc1 = None
        for c in range(BL // step):
            peak0 = scores(0, c, peak0)
        peak0 = jnp.max(peak0, axis=1, keepdims=True)
        for c in range(BL // step):
            peak1 = scores(1, c, peak1)
            acc0 = weigh(0, c, peak0, acc0)
        peak1 = jnp.max(peak1, axis=1, keepdims=True)
        for c in range(BL // step):
            acc1 = weigh(1, c, peak1, acc1)
        lse_rows = finish(0, peak0, acc0) + finish(1, peak1, acc1)
        lsend[pl.ds(base, PT)] = lse_rows.reshape(PT, 1, 128)

        def send_back(i, src, dst, ss, rs):
            p = base + i

            @pl.when(p > 0)
            def _():
                send(src.at[p], dst.at[p], ss, rs, {"ctx": peer(p, -1)})

        pl.loop(0, PT)(lambda i: send_back(i, lsend, lrecv, l_ss, l_rs))
        pl.loop(0, PT)(lambda i: send_back(i, osend, orecv, o_ss, o_rs.at[tile]))

    orecv[0] = osend[0]
    lrecv[0] = lsend[0]

    part = sp.at[pl.ds(0, NX - 1)]
    wait_for(part, b_rs)
    for half in range(2):
        rows = jnp.concatenate([q_ref[0, :, (4 * half + i) * HD:(4 * half + i + 1) * HD] for i in range(4)], axis=0)
        row_pos = me * QD + (iota((RT, 512), 0) & (QD - 1))
        col = iota((RT, 512), 1)

        def own_scores(c):
            key_pos = (col >> 6) * (NX * QD) + c * QD + (col & (QD - 1))
            return jnp.where(key_pos <= row_pos, dot_nt(rows, sp[c, 0]), -1e30)

        values = jnp.concatenate([sp[c, 1] for c in range(NX)], axis=0)
        out, lse = softmax_rows(half, NX * 512, own_scores, values)
        own_o[half * RT:(half + 1) * RT, :] = out
        own_l[0, half * RT:(half + 1) * RT, :] = lse

    wait_for(lrecv.at[pl.ds(0, N - 1)], l_rs)
    pick_jk = own_l[1, 0:TOP * QD, :]
    pick_p = own_l[1, TOP * QD:2 * TOP * QD, 0:N].astype(BF16)
    pieces = jnp.concatenate(split3(lrecv[...].reshape(N, 128)), axis=1)
    picked = dot(pick_p, pieces)
    picked = jnp.concatenate([picked[:, i * 128:(i + 1) * 128] * pick_jk for i in range(3)], axis=1).astype(BF16)
    e0, e1 = iota((3 * 128, GR * HD), 0) & 127, iota((3 * 128, GR * HD), 1)
    spread = jnp.logical_and(e0 < 64, ((e0 >> 2) & 7) == (e1 >> 7)).astype(BF16)
    far_lse = dot(picked, spread)
    for g in range(GR):
        rows = slice(g * QD, (g + 1) * QD)
        lses = [own_l[0, rows, :]] + [far_lse[t * QD:(t + 1) * QD, g * HD:(g + 1) * HD] for t in range(TOP)]
        peak = functools.reduce(jnp.maximum, lses)
        factors = [jnp.exp(v - peak) for v in lses]
        whole = sum(factors)
        own_o[rows, :] = own_o[rows, :] * (factors[0] / whole)
        for t in range(TOP):
            weight[t, rows, :] = factors[t + 1] / whole

    parts = [None, None]
    for tile in range(TILES):
        first = 1 if tile == 0 else 0
        wait_for(orecv.at[pl.ds(first, PT - first)], o_rs.at[tile])
        cols = slice(tile * PT * 16, (tile + 1) * PT * 16)
        for gq in range(2):
            for j in range(JB):
                back = orecv[tile * PT:(tile + 1) * PT, j, gq * 16:(gq + 1) * 16, :].reshape(PT * 16, HD)
                new = dot(ret[j, :, cols], back)
                parts[gq] = new if parts[gq] is None else parts[gq] + new
    for g in range(GR):
        rows = slice(g * QD, (g + 1) * QD)
        mixed = own_o[rows, :]
        for t in range(TOP):
            first = (g % 4 * TOP + t) * QD
            mixed += weight[t, rows, :] * parts[g // 4][first:first + QD]
        att_ref[0, :, g * HD:(g + 1) * HD] = mixed.astype(BF16)

    w_load.wait()
    att = att_ref[0]

    def over_y(c):
        wait_for(r_recv.at[c], r_rs.at[c])
        both = r_stage[core, c].astype(F32) + r_recv[c].astype(F32)
        y_send[c] = both.astype(BF16)

        @pl.loop(1, NY)
        def _(i):
            to = along_y(i)
            send(y_send.at[c, to], y_recv.at[c, i], y_ss, y_rs.at[c], {"kvh": 2 * to + core})

    for c in range(CHUNKS):
        part = dot(att, wbuf[:, c * CW:(c + 1) * CW])
        for k in range(2 * NY):
            rows = part[k * 8:(k + 1) * 8]
            both = jnp.concatenate([rows[:, :CW // 2], rows[:, CW // 2:]], axis=0)
            r_stage[k % 2, c, k // 2] = both.astype(BF16)
        send(r_stage.at[1 - core, c], r_recv.at[c], r_ss, r_rs.at[c], sibling)
        if c > 0:
            over_y(c - 1)
    over_y(CHUNKS - 1)
    for c in range(CHUNKS):
        wait_for(y_recv.at[c, pl.ds(1, NY - 1)], y_rs.at[c])
        total = y_send[c, y].astype(F32)
        for i in range(1, NY):
            total += y_recv[c, i].astype(F32)
        proj_ref[:, c * CW:c * CW + CW // 2] = total[:8].astype(BF16)
        proj_ref[:, c * CW + CW // 2:(c + 1) * CW] = total[8:].astype(BF16)

    for buf, sem in ((qsend, q_ss), (osend, o_ss), (lsend, l_ss)):
        part = buf.at[pl.ds(0, N - 1)]
        wait_for(part, sem)
    part = sp.at[0, :, pl.ds(0, (NZ - 1) * QD), :]
    wait_for(part, a_ss)
    part = sp.at[pl.ds(0, NX - 1)]
    wait_for(part, b_ss)
    wait_for(r_recv, r_ss)
    wait_for(y_recv.at[:, pl.ds(1, NY - 1)], y_ss)


def on_device(queries, span_kv, cache_kv, choices, block_home, out_weight):
    vmem = pl.BlockSpec(memory_space=pltpu.VMEM)
    hbm = pl.BlockSpec(memory_space=pl.ANY)
    dma = pltpu.SemaphoreType.DMA
    attended, projected = pl.pallas_call(
        kernel,
        out_shape=(
            pltpu.VMEM((1, QD, GR * HD), BF16),
            pltpu.VMEM((8, COLS), BF16),
        ),
        in_specs=[hbm] * 6,
        out_specs=(vmem, vmem),
        scratch_shapes=[
            pltpu.VMEM((1, QD, GR * HD), BF16),
            pltpu.VMEM((TOP, 1, 128), jnp.int32),
            pltpu.VMEM((1, NB), jnp.int32),
            pltpu.VMEM((JB, BL, HD), BF16),
            pltpu.VMEM((JB, BL, HD), BF16),
            pltpu.VMEM((GR * HD, COLS), BF16),
            pltpu.VMEM((N, JB, 32, HD), BF16),
            pltpu.VMEM((N, JB, 32, HD), BF16),
            pltpu.VMEM((N, JB, 32, HD), BF16),
            pltpu.VMEM((N, JB, 32, HD), BF16),
            pltpu.VMEM((N, 1, 128), F32),
            pltpu.VMEM((N, 1, 128), F32),
            pltpu.VMEM((NX, 2, NZ * QD, HD), BF16),
            pltpu.VMEM((JB, RT, BL), F32),
            pltpu.VMEM((JB, RT, BL), BF16),
            pltpu.VMEM((JB, 4 * TOP * QD, N * 16), BF16),
            pltpu.VMEM((GR * QD, HD), F32),
            pltpu.VMEM((2, GR * QD, HD), F32),
            pltpu.VMEM((TOP, GR * QD, HD), F32),
            pltpu.VMEM((2, CHUNKS, NY, 16, CW // 2), BF16),
            pltpu.VMEM((CHUNKS, NY, 16, CW // 2), BF16),
            pltpu.VMEM((CHUNKS, NY, 16, CW // 2), BF16),
            pltpu.VMEM((CHUNKS, NY, 16, CW // 2), BF16),
            dma((4,)),
            dma((4,)),
            dma,
            dma,
            dma((TILES,)),
            dma,
            dma((TILES,)),
            dma, dma, dma, dma, dma, dma, dma,
            dma,
            dma((CHUNKS,)),
            dma,
            dma((CHUNKS,)),
        ],
        compiler_params=pltpu.CompilerParams(
            collective_id=0, has_side_effects=True, vmem_limit_bytes=56 * 2**20
        ),
    )(
        queries,
        span_kv,
        cache_kv,
        jnp.transpose(choices, (2, 0, 1)),
        block_home.reshape(1, NB),
        out_weight,
    )
    return attended, projected


def solution(mesh):
    return jax.shard_map(
        on_device,
        mesh=mesh,
        in_specs=(
            P("kvh", "ctx", None),
            P(None, "kvh", "ctx", None),
            P(None, "kvh", "ctx", None),
            P("kvh", None, None),
            P(),
            P("kvh", None),
        ),
        out_specs=(P("kvh", "ctx", None), P(("ctx", "kvh"), None)),
        check_vma=False,
    )
```

```python
import functools
import math

import jax
import jax.numpy as jnp
from jax import lax
from jax.experimental import pallas as pl
from jax.experimental.pallas import tpu as pltpu
from jax.sharding import PartitionSpec as P

MESH = pl.DeviceIdType.MESH
F32 = jnp.float32
BF16 = jnp.bfloat16

NZ, NX, NY = 8, 4, 4
N = NZ * NX
QD = 64
HD = 128
GR = 8
TOP = 3
MOST = 4
NB = 64
BL = 4096
JB = 2
COLS = 4096
CHUNKS = 4
CW = COLS // CHUNKS
TILES = 4
PT = N // TILES
RT = PT * GR * MOST
SCALE = 1.0 / math.sqrt(HD)
EXP2 = SCALE * math.log2(math.e)
NT = (((1,), (1,)), ((), ()))


def iota(shape, dim):
    return lax.broadcasted_iota(jnp.int32, shape, dim)


def dot(a, b):
    return jnp.dot(a, b, preferred_element_type=F32)


def dot_nt(a, b):
    return lax.dot_general(a, b, NT, preferred_element_type=F32)


def offset_of(p):
    dx, i = lax.div(p, NZ), lax.rem(p, NZ)
    return NZ + (2 * lax.rem(i, 2) - 1) * lax.div(i + 1, 2), dx


def offset_vec(p):
    dx, i = p >> 3, p & 7
    return NZ + (2 * (i & 1) - 1) * ((i + 1) >> 1), dx


def one_hots(z, x, home, shape, dim):
    n = iota(shape, dim)
    dz, dx = offset_vec(n >> 4)
    dest = (((z + dz) & (NZ - 1)) << 2) | ((x + dx) & (NX - 1))
    return [(home == dest * JB + j).astype(BF16) for j in range(JB)]


def send(src, dst, ss, rs, who):
    pltpu.make_async_remote_copy(src, dst, ss, rs, device_id=who, device_id_type=MESH).start()


def wait_for(part, sem):
    pltpu.make_async_copy(part, part, sem).wait()


def split3(v):
    hi = v.astype(BF16)
    rest = v - hi.astype(F32)
    mid = rest.astype(BF16)
    return hi, mid, (rest - mid.astype(F32)).astype(BF16)


def kernel(
    q_hbm, span_ref, cache_ref, ch_hbm, home_hbm, w_ref, att_ref, proj_ref,
    q_ref, ch_ref, home_ref, kbuf, vbuf, wbuf, qsend, qrecv, osend, orecv, lsend, lrecv, sp, s_scr, ret, own_o, own_l, weight, r_stage, r_recv, y_send, y_recv,
    isem, lsem, wsem, q_ss, q_rs, o_ss, o_rs, l_ss, l_rs, a_ss, a_rs, a2_rs, b_ss, b_rs, r_ss, r_rs, y_ss, y_rs,
):
    me = lax.axis_index("ctx")
    kv = lax.axis_index("kvh")
    z, x = lax.div(me, NX), lax.rem(me, NX)

    def peer(p, sign=1):
        dz, dx = offset_of(p)
        if sign < 0:
            dz, dx = 2 * NZ - dz, NX - dx
        return lax.rem(z + dz, NZ) * NX + lax.rem(x + dx, NX)

    barrier = pltpu.get_barrier_semaphore()

    @pl.loop(1, N)
    def _(p):
        pl.semaphore_signal(barrier, inc=1, device_id={"ctx": peer(p)}, device_id_type=MESH)

    core, y = lax.rem(kv, 2), lax.div(kv, 2)
    sibling = {"kvh": kv + 1 - 2 * core}

    def along_y(i):
        return lax.rem(y + i, NY)

    pl.semaphore_signal(barrier, inc=1, device_id=sibling, device_id_type=MESH)

    @pl.loop(1, NY)
    def _(i):
        pl.semaphore_signal(barrier, inc=1, device_id={"kvh": 2 * along_y(i) + core}, device_id_type=MESH)

    mine_z = sp.at[x, :, pl.ds(pl.multiple_of(z * QD, QD), QD), :]
    pair = pl.ds(pl.multiple_of(lax.div(me, 2) * 128, 128), 128)
    inputs = [
        pltpu.make_async_copy(span_ref.at[:, 0], mine_z, isem.at[0]),
        pltpu.make_async_copy(ch_hbm.at[:, :, pair], ch_ref, isem.at[1]),
        pltpu.make_async_copy(home_hbm, home_ref, isem.at[2]),
        pltpu.make_async_copy(q_hbm, q_ref, isem.at[3]),
    ]
    for load in inputs:
        load.start()
    loads = []
    for j in range(JB):
        rows = pl.ds(j * BL, BL)
        loads.append(pltpu.make_async_copy(cache_ref.at[0, 0, rows], kbuf.at[j], lsem.at[2 * j]))
        loads.append(pltpu.make_async_copy(cache_ref.at[1, 0, rows], vbuf.at[j], lsem.at[2 * j + 1]))
    w_load = pltpu.make_async_copy(w_ref, wbuf, wsem)
    for load in loads:
        load.start()
    w_load.start()

    inputs[0].wait()
    pl.semaphore_wait(barrier, N - 1 + 1 + NY - 1)

    def at_z(d):
        return lax.rem(z + NZ + d, NZ)

    def send_z(src, sem, d):
        send(src, src, a_ss, sem, {"ctx": at_z(d) * NX + x})

    for d in (2, -2):
        send_z(mine_z, a_rs, d)
    for d in (1, -1):
        send_z(mine_z, a2_rs, d)

    for load in inputs[1:]:
        load.wait()
    width = 4 * QD
    lanes = iota((1, 128), 1)
    c4 = []
    for t in range(TOP):
        v = ch_ref[t]
        mine = jnp.where((lanes >> 6) == lax.rem(me, 2), v, jnp.concatenate([v[:, QD:], v[:, :QD]], axis=1))
        c4.append(jnp.concatenate([mine, mine], axis=1))
    chosen = functools.reduce(jnp.logical_or, [iota((NB, width), 0) == c for c in c4]).astype(BF16)
    home = home_ref[...]
    nrow = PT * TILES * 16
    places = one_hots(z, x, home, (nrow, 1), 0)
    r0, r1 = iota((width, width), 0), iota((width, width), 1)
    earlier = jnp.logical_and((r0 >> 6) == (r1 >> 6), r0 < r1).astype(BF16)
    rown = iota((nrow, width), 0)
    keep_gg = ((rown >> 2) & 3) == (iota((nrow, width), 1) >> 6)
    rank_n = (rown & 3).astype(F32)
    q = q_ref[0]
    stacked = [
        jnp.concatenate([q[:, (4 * gq + gg) * HD:(4 * gq + gg + 1) * HD] for gg in range(4)], axis=0)
        for gq in range(2)
    ]
    for j in range(JB):
        here = dot(places[j], chosen)
        rank = dot(here.astype(BF16), earlier)
        pick = jnp.where(jnp.logical_and(keep_gg, rank == rank_n), here, 0.0).astype(BF16)
        for gq in range(2):
            rows = dot(pick, stacked[gq]).astype(BF16).reshape(N, 16, HD)
            qsend[:, j, gq * 16:(gq + 1) * 16, :] = rows

    qrecv[0] = qsend[0]

    def send_rows(p):
        send(qsend.at[p], qrecv.at[p], q_ss, q_rs.at[lax.div(p, PT)], {"ctx": peer(p)})

    pl.loop(1, PT)(send_rows)

    wait_for(sp.at[0, :, pl.ds(0, 2 * QD), :], a_rs)
    below = pl.ds(pl.multiple_of(at_z(-2) * QD, QD), QD)
    above = pl.ds(pl.multiple_of(at_z(2) * QD, QD), QD)
    send_z(sp.at[x, :, below], a2_rs, 1)
    send_z(sp.at[x, :, above], a2_rs, -1)
    send_z(sp.at[x, 0, below], a2_rs, 2)
    send_z(sp.at[x, 1, above], a2_rs, -2)

    pl.loop(PT, N)(send_rows)

    c8 = jnp.concatenate(c4 + [jnp.zeros((8 - TOP, width), jnp.int32)], axis=0).astype(F32).T
    place_n = one_hots(z, x, home, (nrow, 1), 0)
    keep_t = (iota((width, nrow), 0) >> 6) == ((iota((width, nrow), 1) >> 2) & 3)
    rank_t = (iota((width, nrow), 1) & 3).astype(F32)
    later = jnp.logical_and((r0 >> 6) == (r1 >> 6), r1 < r0).astype(BF16)
    blocks = iota((width, NB), 1).astype(F32)
    one_t = [(c8[:, t:t + 1] == blocks).astype(BF16) for t in range(TOP)]
    any_t = one_t[0] + one_t[1] + one_t[2]
    f0, f1 = iota((nrow, 128), 0), iota((nrow, 128), 1)
    first_gg = ((f0 >> 2) & 3) == 0
    by_p = jnp.logical_and(first_gg, (f0 >> 4) == f1).astype(BF16)
    pick_p = [None] * TOP
    pick_jk = [None] * TOP
    for j in range(JB):
        rank = dot(later, dot_nt(any_t, place_n[j]).astype(BF16))
        keep = jnp.logical_and(keep_t, rank == rank_t)
        to_lane = jnp.logical_and(
            jnp.logical_and(first_gg, (f1 >> 5) == j), (f0 & 3) == (f1 & 3)
        ).astype(BF16)
        for t in range(TOP):
            pick = jnp.where(keep, dot_nt(one_t[t], place_n[j]), 0.0).astype(BF16)
            for gg in range(4):
                ret[j, pl.ds((gg * TOP + t) * QD, QD), :] = pick[gg * QD:(gg + 1) * QD]
            part_p, part_jk = dot(pick[:QD], by_p), dot(pick[:QD], to_lane)
            pick_p[t] = part_p if j == 0 else pick_p[t] + part_p
            pick_jk[t] = part_jk if j == 0 else pick_jk[t] + part_jk
    pick_p = jnp.concatenate(pick_p, axis=0).astype(BF16)
    pick_jk = jnp.concatenate(pick_jk, axis=0)
    own_l[1, 0:TOP * QD, :] = pick_jk
    own_l[1, TOP * QD:2 * TOP * QD, :] = pick_p.astype(F32)

    ones = jnp.ones((BL, HD), BF16)

    for load in loads:
        load.wait()

    wait_for(sp.at[0, :, pl.ds(0, 5 * QD), :], a2_rs)

    @pl.loop(1, NX)
    def _(i):
        send(sp.at[x], sp.at[x], b_ss, b_rs.at[i], {"ctx": z * NX + lax.rem(x + i, NX)})

    lane_of = iota((RT, 128), 1)
    row_in = iota((RT, 128), 0) & 31

    @pl.loop(0, TILES)
    def _(tile):
        @pl.when(tile == 0)
        def _():
            part = qrecv.at[pl.ds(0, PT - 1)]
            wait_for(part, q_rs.at[0])

        @pl.when(tile > 0)
        def _():
            part = qrecv.at[pl.ds(0, PT)]
            wait_for(part, q_rs.at[tile])

        base = tile * PT
        lse_rows = jnp.zeros((PT, 128), F32)
        step = 512
        rows = [qrecv[pl.ds(base, PT), j].reshape(RT, HD) for j in range(JB)]

        def scores(j, c, peak):
            s = dot_nt(rows[j], kbuf[j, c * step:(c + 1) * step, :])
            s_scr[j, :, c * step:(c + 1) * step] = s
            for i in range(step // 128):
                piece = s[:, i * 128:(i + 1) * 128]
                peak = piece if peak is None else jnp.maximum(peak, piece)
            return peak

        def weigh(j, c, peak, acc):
            cols = slice(c * step, (c + 1) * step)
            p = jnp.exp2((s_scr[j, :, cols] - peak) * EXP2).astype(BF16)
            new = dot(p, jnp.concatenate([vbuf[j, cols], ones[cols]], axis=1))
            return new if acc is None else acc + new

        def finish(j, peak, acc):
            total = acc[:, HD:]
            osend[pl.ds(base, PT), j] = (acc[:, :HD] / total).astype(BF16).reshape(PT, 32, HD)
            lse = jnp.where(lane_of == row_in + j * 32, peak * SCALE + jnp.log(total), 0.0)
            return jnp.sum(lse.reshape(PT, 32, 128), axis=1)

        peak0 = peak1 = acc0 = acc1 = None
        for c in range(BL // step):
            peak0 = scores(0, c, peak0)
        peak0 = jnp.max(peak0, axis=1, keepdims=True)
        for c in range(BL // step):
            peak1 = scores(1, c, peak1)
            acc0 = weigh(0, c, peak0, acc0)
        peak1 = jnp.max(peak1, axis=1, keepdims=True)
        for c in range(BL // step):
            acc1 = weigh(1, c, peak1, acc1)
        lse_rows = finish(0, peak0, acc0) + finish(1, peak1, acc1)
        lsend[pl.ds(base, PT)] = lse_rows.reshape(PT, 1, 128)

        def send_back(i, src, dst, ss, rs):
            p = base + i

            @pl.when(p > 0)
            def _():
                send(src.at[p], dst.at[p], ss, rs, {"ctx": peer(p, -1)})

        pl.loop(0, PT)(lambda i: send_back(i, lsend, lrecv, l_ss, l_rs))
        pl.loop(0, PT)(lambda i: send_back(i, osend, orecv, o_ss, o_rs.at[tile]))

    orecv[0] = osend[0]
    lrecv[0] = lsend[0]

    own_rows = [
        jnp.concatenate([q_ref[0, :, (4 * h + i) * HD:(4 * h + i + 1) * HD] for i in range(4)], axis=0)
        for h in range(2)
    ]
    step = NZ * QD
    row_pos = me * QD + (iota((RT, step), 0) & (QD - 1))
    col = iota((RT, step), 1)
    key_pos = (col >> 6) * (NX * QD) + (col & (QD - 1))

    xs = [lax.rem(x + NX - c, NX) for c in range(NX)]

    def own_scores(h, c, peak):
        s = jnp.where(key_pos + xs[c] * QD <= row_pos, dot_nt(own_rows[h], sp[xs[c], 0]), -1e30)
        s_scr[h, :, c * step:(c + 1) * step] = s
        for i in range(step // 128):
            piece = s[:, i * 128:(i + 1) * 128]
            peak = piece if peak is None else jnp.maximum(peak, piece)
        return peak

    def own_weigh(h, c, peak, acc):
        p = jnp.exp2((s_scr[h, :, c * step:(c + 1) * step] - peak) * EXP2).astype(BF16)
        new = dot(p, jnp.concatenate([sp[xs[c], 1], ones[:step]], axis=1))
        return new if acc is None else acc + new

    peaks, accs = [None, None], [None, None]
    for c in range(NX):
        if c > 0:
            wait_for(sp.at[0], b_rs.at[c])
        for h in range(2):
            peaks[h] = own_scores(h, c, peaks[h])
    for h in range(2):
        peaks[h] = jnp.max(peaks[h], axis=1, keepdims=True)
        for c in range(NX):
            accs[h] = own_weigh(h, c, peaks[h], accs[h])
    for h in range(2):
        total = accs[h][:, HD:]
        own_o[h * RT:(h + 1) * RT, :] = accs[h][:, :HD] / total
        own_l[0, h * RT:(h + 1) * RT, :] = peaks[h] * SCALE + jnp.log(total)

    wait_for(lrecv.at[pl.ds(0, N - 1)], l_rs)
    pick_jk = own_l[1, 0:TOP * QD, :]
    pick_p = own_l[1, TOP * QD:2 * TOP * QD, 0:N].astype(BF16)
    pieces = jnp.concatenate(split3(lrecv[...].reshape(N, 128)), axis=1)
    picked = dot(pick_p, pieces)
    picked = jnp.concatenate([picked[:, i * 128:(i + 1) * 128] * pick_jk for i in range(3)], axis=1).astype(BF16)
    e0, e1 = iota((3 * 128, GR * HD), 0) & 127, iota((3 * 128, GR * HD), 1)
    spread = jnp.logical_and(e0 < 64, ((e0 >> 2) & 7) == (e1 >> 7)).astype(BF16)
    far_lse = dot(picked, spread)
    for g in range(GR):
        rows = slice(g * QD, (g + 1) * QD)
        lses = [own_l[0, rows, :]] + [far_lse[t * QD:(t + 1) * QD, g * HD:(g + 1) * HD] for t in range(TOP)]
        peak = functools.reduce(jnp.maximum, lses)
        factors = [jnp.exp(v - peak) for v in lses]
        whole = sum(factors)
        own_o[rows, :] = own_o[rows, :] * (factors[0] / whole)
        for t in range(TOP):
            weight[t, rows, :] = factors[t + 1] / whole

    parts = [None, None]
    for tile in range(TILES):
        first = 1 if tile == 0 else 0
        wait_for(orecv.at[pl.ds(first, PT - first)], o_rs.at[tile])
        cols = slice(tile * PT * 16, (tile + 1) * PT * 16)
        for gq in range(2):
            for j in range(JB):
                back = orecv[tile * PT:(tile + 1) * PT, j, gq * 16:(gq + 1) * 16, :].reshape(PT * 16, HD)
                new = dot(ret[j, :, cols], back)
                parts[gq] = new if parts[gq] is None else parts[gq] + new
    for g in range(GR):
        rows = slice(g * QD, (g + 1) * QD)
        mixed = own_o[rows, :]
        for t in range(TOP):
            first = (g % 4 * TOP + t) * QD
            mixed += weight[t, rows, :] * parts[g // 4][first:first + QD]
        att_ref[0, :, g * HD:(g + 1) * HD] = mixed.astype(BF16)

    w_load.wait()
    att = att_ref[0]

    def over_y(c):
        wait_for(r_recv.at[c], r_rs.at[c])
        both = r_stage[core, c].astype(F32) + r_recv[c].astype(F32)
        y_send[c] = both.astype(BF16)

        @pl.loop(1, NY)
        def _(i):
            to = along_y(i)
            send(y_send.at[c, to], y_recv.at[c, i], y_ss, y_rs.at[c], {"kvh": 2 * to + core})

    for c in range(CHUNKS):
        part = dot(att, wbuf[:, c * CW:(c + 1) * CW])
        for k in range(2 * NY):
            rows = part[k * 8:(k + 1) * 8]
            both = jnp.concatenate([rows[:, :CW // 2], rows[:, CW // 2:]], axis=0)
            r_stage[k % 2, c, k // 2] = both.astype(BF16)
        send(r_stage.at[1 - core, c], r_recv.at[c], r_ss, r_rs.at[c], sibling)
        if c > 0:
            over_y(c - 1)
    over_y(CHUNKS - 1)
    for c in range(CHUNKS):
        wait_for(y_recv.at[c, pl.ds(1, NY - 1)], y_rs.at[c])
        total = y_send[c, y].astype(F32)
        for i in range(1, NY):
            total += y_recv[c, i].astype(F32)
        proj_ref[:, c * CW:c * CW + CW // 2] = total[:8].astype(BF16)
        proj_ref[:, c * CW + CW // 2:(c + 1) * CW] = total[8:].astype(BF16)

    for buf, sem in ((qsend, q_ss), (osend, o_ss), (lsend, l_ss)):
        part = buf.at[pl.ds(0, N - 1)]
        wait_for(part, sem)
    part = sp.at[0, :, pl.ds(0, (NZ - 1) * QD), :]
    wait_for(part, a_ss)
    part = sp.at[pl.ds(0, NX - 1)]
    wait_for(part, b_ss)
    wait_for(r_recv, r_ss)
    wait_for(y_recv.at[:, pl.ds(1, NY - 1)], y_ss)


def on_device(queries, span_kv, cache_kv, choices, block_home, out_weight):
    vmem = pl.BlockSpec(memory_space=pltpu.VMEM)
    hbm = pl.BlockSpec(memory_space=pl.ANY)
    dma = pltpu.SemaphoreType.DMA
    attended, projected = pl.pallas_call(
        kernel,
        out_shape=(
            pltpu.VMEM((1, QD, GR * HD), BF16),
            pltpu.VMEM((8, COLS), BF16),
        ),
        in_specs=[hbm] * 6,
        out_specs=(vmem, vmem),
        scratch_shapes=[
            pltpu.VMEM((1, QD, GR * HD), BF16),
            pltpu.VMEM((TOP, 1, 128), jnp.int32),
            pltpu.VMEM((1, NB), jnp.int32),
            pltpu.VMEM((JB, BL, HD), BF16),
            pltpu.VMEM((JB, BL, HD), BF16),
            pltpu.VMEM((GR * HD, COLS), BF16),
            pltpu.VMEM((N, JB, 32, HD), BF16),
            pltpu.VMEM((N, JB, 32, HD), BF16),
            pltpu.VMEM((N, JB, 32, HD), BF16),
            pltpu.VMEM((N, JB, 32, HD), BF16),
            pltpu.VMEM((N, 1, 128), F32),
            pltpu.VMEM((N, 1, 128), F32),
            pltpu.VMEM((NX, 2, NZ * QD, HD), BF16),
            pltpu.VMEM((JB, RT, BL), F32),
            pltpu.VMEM((JB, 4 * TOP * QD, N * 16), BF16),
            pltpu.VMEM((GR * QD, HD), F32),
            pltpu.VMEM((2, GR * QD, HD), F32),
            pltpu.VMEM((TOP, GR * QD, HD), F32),
            pltpu.VMEM((2, CHUNKS, NY, 16, CW // 2), BF16),
            pltpu.VMEM((CHUNKS, NY, 16, CW // 2), BF16),
            pltpu.VMEM((CHUNKS, NY, 16, CW // 2), BF16),
            pltpu.VMEM((CHUNKS, NY, 16, CW // 2), BF16),
            dma((4,)),
            dma((4,)),
            dma,
            dma,
            dma((TILES,)),
            dma,
            dma((TILES,)),
            dma, dma, dma, dma, dma, dma,
            dma((NX,)),
            dma,
            dma((CHUNKS,)),
            dma,
            dma((CHUNKS,)),
        ],
        compiler_params=pltpu.CompilerParams(
            collective_id=0, has_side_effects=True, vmem_limit_bytes=56 * 2**20
        ),
    )(
        queries,
        span_kv,
        cache_kv,
        jnp.transpose(choices, (2, 0, 1)),
        block_home.reshape(1, NB),
        out_weight,
    )
    return attended, projected


def solution(mesh):
    return jax.shard_map(
        on_device,
        mesh=mesh,
        in_specs=(
            P("kvh", "ctx", None),
            P(None, "kvh", "ctx", None),
            P(None, "kvh", "ctx", None),
            P("kvh", None, None),
            P(),
            P("kvh", None),
        ),
        out_specs=(P("kvh", "ctx", None), P(("ctx", "kvh"), None)),
        check_vma=False,
    )
```

```python
import functools
import math

import jax
import jax.numpy as jnp
from jax import lax
from jax.experimental import pallas as pl
from jax.experimental.pallas import tpu as pltpu
from jax.sharding import PartitionSpec as P

MESH = pl.DeviceIdType.MESH
F32 = jnp.float32
BF16 = jnp.bfloat16

NZ, NX, NY = 8, 4, 4
N = NZ * NX
QD = 64
HD = 128
GR = 8
TOP = 3
MOST = 4
NB = 64
BL = 4096
JB = 2
COLS = 4096
CHUNKS = 4
CW = COLS // CHUNKS
TILES = 4
PT = N // TILES
RT = PT * GR * MOST
SCALE = 1.0 / math.sqrt(HD)
EXP2 = SCALE * math.log2(math.e)
NT = (((1,), (1,)), ((), ()))


def iota(shape, dim):
    return lax.broadcasted_iota(jnp.int32, shape, dim)


def dot(a, b):
    return jnp.dot(a, b, preferred_element_type=F32)


def dot_nt(a, b):
    return lax.dot_general(a, b, NT, preferred_element_type=F32)


def offset_of(p):
    dx, i = lax.div(p, NZ), lax.rem(p, NZ)
    return NZ + (2 * lax.rem(i, 2) - 1) * lax.div(i + 1, 2), dx


def offset_vec(p):
    dx, i = p >> 3, p & 7
    return NZ + (2 * (i & 1) - 1) * ((i + 1) >> 1), dx


def one_hots(z, x, home, shape, dim):
    n = iota(shape, dim)
    dz, dx = offset_vec(n >> 4)
    dest = (((z + dz) & (NZ - 1)) << 2) | ((x + dx) & (NX - 1))
    return [(home == dest * JB + j).astype(BF16) for j in range(JB)]


def send(src, dst, ss, rs, who):
    pltpu.make_async_remote_copy(src, dst, ss, rs, device_id=who, device_id_type=MESH).start()


def wait_for(part, sem):
    pltpu.make_async_copy(part, part, sem).wait()


def split3(v):
    hi = v.astype(BF16)
    rest = v - hi.astype(F32)
    mid = rest.astype(BF16)
    return hi, mid, (rest - mid.astype(F32)).astype(BF16)


def kernel(
    q_hbm, span_ref, cache_ref, ch_hbm, home_hbm, w_ref, att_ref, proj_ref,
    q_ref, ch_ref, home_ref, kbuf, vbuf, wbuf, qsend, qrecv, osend, orecv, lsend, lrecv, sp, s_scr, ret, own_o, own_l, weight, r_stage, r_recv, y_send, y_recv,
    isem, lsem, wsem, q_ss, q_rs, o_ss, o_rs, l_ss, l_rs, a_ss, a_rs, a2_rs, b_ss, b_rs, r_ss, r_rs, y_ss, y_rs,
):
    me = lax.axis_index("ctx")
    kv = lax.axis_index("kvh")
    z, x = lax.div(me, NX), lax.rem(me, NX)

    def peer(p, sign=1):
        dz, dx = offset_of(p)
        if sign < 0:
            dz, dx = 2 * NZ - dz, NX - dx
        return lax.rem(z + dz, NZ) * NX + lax.rem(x + dx, NX)

    barrier = pltpu.get_barrier_semaphore()

    @pl.loop(1, N)
    def _(p):
        pl.semaphore_signal(barrier, inc=1, device_id={"ctx": peer(p)}, device_id_type=MESH)

    core, y = lax.rem(kv, 2), lax.div(kv, 2)
    sibling = {"kvh": kv + 1 - 2 * core}

    def along_y(i):
        return lax.rem(y + i, NY)

    pl.semaphore_signal(barrier, inc=1, device_id=sibling, device_id_type=MESH)

    @pl.loop(1, NY)
    def _(i):
        pl.semaphore_signal(barrier, inc=1, device_id={"kvh": 2 * along_y(i) + core}, device_id_type=MESH)

    mine_z = sp.at[x, :, pl.ds(pl.multiple_of(z * QD, QD), QD), :]
    pair = pl.ds(pl.multiple_of(lax.div(me, 2) * 128, 128), 128)
    inputs = [
        pltpu.make_async_copy(span_ref.at[:, 0], mine_z, isem.at[0]),
        pltpu.make_async_copy(ch_hbm.at[:, :, pair], ch_ref, isem.at[1]),
        pltpu.make_async_copy(home_hbm, home_ref, isem.at[2]),
        pltpu.make_async_copy(q_hbm, q_ref, isem.at[3]),
    ]
    for load in inputs:
        load.start()
    loads = []
    for j in range(JB):
        rows = pl.ds(j * BL, BL)
        loads.append(pltpu.make_async_copy(cache_ref.at[0, 0, rows], kbuf.at[j], lsem.at[2 * j]))
        loads.append(pltpu.make_async_copy(cache_ref.at[1, 0, rows], vbuf.at[j], lsem.at[2 * j + 1]))
    w_load = pltpu.make_async_copy(w_ref, wbuf, wsem)
    for load in loads:
        load.start()
    w_load.start()

    inputs[0].wait()
    pl.semaphore_wait(barrier, N - 1 + 1 + NY - 1)

    def at_z(d):
        return lax.rem(z + NZ + d, NZ)

    def send_z(src, sem, d):
        send(src, src, a_ss, sem, {"ctx": at_z(d) * NX + x})

    for d in (2, -2):
        send_z(mine_z, a_rs, d)
    for d in (1, -1):
        send_z(mine_z, a2_rs, d)

    for load in inputs[1:]:
        load.wait()
    width = 4 * QD
    lanes = iota((1, 128), 1)
    c4 = []
    for t in range(TOP):
        v = ch_ref[t]
        mine = jnp.where((lanes >> 6) == lax.rem(me, 2), v, jnp.concatenate([v[:, QD:], v[:, :QD]], axis=1))
        c4.append(jnp.concatenate([mine, mine], axis=1))
    chosen = functools.reduce(jnp.logical_or, [iota((NB, width), 0) == c for c in c4]).astype(BF16)
    home = home_ref[...]
    nrow = PT * TILES * 16
    places = one_hots(z, x, home, (nrow, 1), 0)
    r0, r1 = iota((width, width), 0), iota((width, width), 1)
    earlier = jnp.logical_and((r0 >> 6) == (r1 >> 6), r0 < r1).astype(BF16)
    rown = iota((nrow, width), 0)
    keep_gg = ((rown >> 2) & 3) == (iota((nrow, width), 1) >> 6)
    rank_n = (rown & 3).astype(F32)
    q = q_ref[0]
    stacked = [
        jnp.concatenate([q[:, (4 * gq + gg) * HD:(4 * gq + gg + 1) * HD] for gg in range(4)], axis=0)
        for gq in range(2)
    ]
    for j in range(JB):
        here = dot(places[j], chosen)
        rank = dot(here.astype(BF16), earlier)
        pick = jnp.where(jnp.logical_and(keep_gg, rank == rank_n), here, 0.0).astype(BF16)
        for gq in range(2):
            rows = dot(pick, stacked[gq]).astype(BF16).reshape(N, 16, HD)
            qsend[:, j, gq * 16:(gq + 1) * 16, :] = rows

    qrecv[0] = qsend[0]

    def send_rows(p):
        send(qsend.at[p], qrecv.at[p], q_ss, q_rs.at[lax.div(p, PT)], {"ctx": peer(p)})

    pl.loop(1, PT)(send_rows)

    wait_for(sp.at[0, :, pl.ds(0, 2 * QD), :], a_rs)
    below = pl.ds(pl.multiple_of(at_z(-2) * QD, QD), QD)
    above = pl.ds(pl.multiple_of(at_z(2) * QD, QD), QD)
    send_z(sp.at[x, :, below], a2_rs, 1)
    send_z(sp.at[x, :, above], a2_rs, -1)
    send_z(sp.at[x, 0, below], a2_rs, 2)
    send_z(sp.at[x, 1, above], a2_rs, -2)

    pl.loop(PT, N)(send_rows)

    c8 = jnp.concatenate(c4 + [jnp.zeros((8 - TOP, width), jnp.int32)], axis=0).astype(F32).T
    place_n = one_hots(z, x, home, (nrow, 1), 0)
    keep_t = (iota((width, nrow), 0) >> 6) == ((iota((width, nrow), 1) >> 2) & 3)
    rank_t = (iota((width, nrow), 1) & 3).astype(F32)
    later = jnp.logical_and((r0 >> 6) == (r1 >> 6), r1 < r0).astype(BF16)
    blocks = iota((width, NB), 1).astype(F32)
    one_t = [(c8[:, t:t + 1] == blocks).astype(BF16) for t in range(TOP)]
    any_t = one_t[0] + one_t[1] + one_t[2]
    f0, f1 = iota((nrow, 128), 0), iota((nrow, 128), 1)
    first_gg = ((f0 >> 2) & 3) == 0
    by_p = jnp.logical_and(first_gg, (f0 >> 4) == f1).astype(BF16)
    pick_p = [None] * TOP
    pick_jk = [None] * TOP
    for j in range(JB):
        rank = dot(later, dot_nt(any_t, place_n[j]).astype(BF16))
        keep = jnp.logical_and(keep_t, rank == rank_t)
        to_lane = jnp.logical_and(
            jnp.logical_and(first_gg, (f1 >> 5) == j), (f0 & 3) == (f1 & 3)
        ).astype(BF16)
        for t in range(TOP):
            pick = jnp.where(keep, dot_nt(one_t[t], place_n[j]), 0.0).astype(BF16)
            for gg in range(4):
                ret[j, pl.ds((gg * TOP + t) * QD, QD), :] = pick[gg * QD:(gg + 1) * QD]
            part_p, part_jk = dot(pick[:QD], by_p), dot(pick[:QD], to_lane)
            pick_p[t] = part_p if j == 0 else pick_p[t] + part_p
            pick_jk[t] = part_jk if j == 0 else pick_jk[t] + part_jk
    pick_p = jnp.concatenate(pick_p, axis=0).astype(BF16)
    pick_jk = jnp.concatenate(pick_jk, axis=0)
    own_l[1, 0:TOP * QD, :] = pick_jk
    own_l[1, TOP * QD:2 * TOP * QD, :] = pick_p.astype(F32)

    ones = jnp.ones((BL, HD), BF16)

    for load in loads:
        load.wait()

    wait_for(sp.at[0, :, pl.ds(0, 5 * QD), :], a2_rs)

    @pl.loop(1, NX)
    def _(i):
        send(sp.at[x], sp.at[x], b_ss, b_rs.at[i], {"ctx": z * NX + lax.rem(x + i, NX)})

    lane_of = iota((RT, 128), 1)
    row_in = iota((RT, 128), 0) & 31

    @pl.loop(0, TILES)
    def _(tile):
        @pl.when(tile == 0)
        def _():
            part = qrecv.at[pl.ds(0, PT - 1)]
            wait_for(part, q_rs.at[0])

        @pl.when(tile > 0)
        def _():
            part = qrecv.at[pl.ds(0, PT)]
            wait_for(part, q_rs.at[tile])

        base = tile * PT
        lse_rows = jnp.zeros((PT, 128), F32)
        step = 512
        rows = [qrecv[pl.ds(base, PT), j].reshape(RT, HD) for j in range(JB)]

        def scores(j, c, peak):
            s = dot_nt(rows[j], kbuf[j, c * step:(c + 1) * step, :])
            s_scr[j, :, c * step:(c + 1) * step] = s
            for i in range(step // 128):
                piece = s[:, i * 128:(i + 1) * 128]
                peak = piece if peak is None else jnp.maximum(peak, piece)
            return peak

        def weigh(j, c, peak, acc):
            cols = slice(c * step, (c + 1) * step)
            p = jnp.exp2((s_scr[j, :, cols] - peak) * EXP2).astype(BF16)
            new = dot(p, jnp.concatenate([vbuf[j, cols], ones[cols]], axis=1))
            return new if acc is None else acc + new

        def finish(j, peak, acc):
            total = acc[:, HD:]
            osend[pl.ds(base, PT), j] = (acc[:, :HD] / total).astype(BF16).reshape(PT, 32, HD)
            lse = jnp.where(lane_of == row_in + j * 32, peak * SCALE + jnp.log(total), 0.0)
            return jnp.sum(lse.reshape(PT, 32, 128), axis=1)

        peak0 = peak1 = acc0 = acc1 = None
        for c in range(BL // step):
            peak0 = scores(0, c, peak0)
        peak0 = jnp.max(peak0, axis=1, keepdims=True)
        for c in range(BL // step):
            peak1 = scores(1, c, peak1)
            acc0 = weigh(0, c, peak0, acc0)
        peak1 = jnp.max(peak1, axis=1, keepdims=True)
        for c in range(BL // step):
            acc1 = weigh(1, c, peak1, acc1)
        lse_rows = finish(0, peak0, acc0) + finish(1, peak1, acc1)
        lsend[pl.ds(base, PT)] = lse_rows.reshape(PT, 1, 128)

        def send_back(i, src, dst, ss, rs):
            p = base + i

            @pl.when(p > 0)
            def _():
                send(src.at[p], dst.at[p], ss, rs, {"ctx": peer(p, -1)})

        pl.loop(0, PT)(lambda i: send_back(i, lsend, lrecv, l_ss, l_rs))
        pl.loop(0, PT)(lambda i: send_back(i, osend, orecv, o_ss, o_rs.at[tile]))

    orecv[0] = osend[0]
    lrecv[0] = lsend[0]

    own_rows = [
        jnp.concatenate([q_ref[0, :, (4 * h + i) * HD:(4 * h + i + 1) * HD] for i in range(4)], axis=0)
        for h in range(2)
    ]
    step = NZ * QD
    row_pos = me * QD + (iota((RT, step), 0) & (QD - 1))
    col = iota((RT, step), 1)
    key_pos = (col >> 6) * (NX * QD) + (col & (QD - 1))

    xs = [lax.rem(x + NX - c, NX) for c in range(NX)]

    def own_scores(h, c, peak):
        s = jnp.where(key_pos + xs[c] * QD <= row_pos, dot_nt(own_rows[h], sp[xs[c], 0]), -1e30)
        s_scr[h, :, c * step:(c + 1) * step] = s
        for i in range(step // 128):
            piece = s[:, i * 128:(i + 1) * 128]
            peak = piece if peak is None else jnp.maximum(peak, piece)
        return peak

    def own_weigh(h, c, peak, acc):
        p = jnp.exp2((s_scr[h, :, c * step:(c + 1) * step] - peak) * EXP2).astype(BF16)
        new = dot(p, jnp.concatenate([sp[xs[c], 1], ones[:step]], axis=1))
        return new if acc is None else acc + new

    peaks, accs = [None, None], [None, None]
    for c in range(NX):
        if c > 0:
            wait_for(sp.at[0], b_rs.at[c])
        for h in range(2):
            peaks[h] = own_scores(h, c, peaks[h])
    for h in range(2):
        peaks[h] = jnp.max(peaks[h], axis=1, keepdims=True)
        for c in range(NX):
            accs[h] = own_weigh(h, c, peaks[h], accs[h])
    for h in range(2):
        total = accs[h][:, HD:]
        own_o[h * RT:(h + 1) * RT, :] = accs[h][:, :HD] / total
        own_l[0, h * RT:(h + 1) * RT, :] = peaks[h] * SCALE + jnp.log(total)

    wait_for(lrecv.at[pl.ds(0, N - 1)], l_rs)
    pick_jk = own_l[1, 0:TOP * QD, :]
    pick_p = own_l[1, TOP * QD:2 * TOP * QD, 0:N].astype(BF16)
    pieces = jnp.concatenate(split3(lrecv[...].reshape(N, 128)), axis=1)
    picked = dot(pick_p, pieces)
    picked = jnp.concatenate([picked[:, i * 128:(i + 1) * 128] * pick_jk for i in range(3)], axis=1).astype(BF16)
    e0, e1 = iota((3 * 128, GR * HD), 0) & 127, iota((3 * 128, GR * HD), 1)
    spread = jnp.logical_and(e0 < 64, ((e0 >> 2) & 7) == (e1 >> 7)).astype(BF16)
    far_lse = dot(picked, spread)
    for g in range(GR):
        rows = slice(g * QD, (g + 1) * QD)
        lses = [own_l[0, rows, :]] + [far_lse[t * QD:(t + 1) * QD, g * HD:(g + 1) * HD] for t in range(TOP)]
        peak = functools.reduce(jnp.maximum, lses)
        factors = [jnp.exp(v - peak) for v in lses]
        whole = sum(factors)
        own_o[rows, :] = own_o[rows, :] * (factors[0] / whole)
        for t in range(TOP):
            weight[t, rows, :] = factors[t + 1] / whole

    parts = [None, None]
    for tile in range(TILES):
        first = 1 if tile == 0 else 0
        wait_for(orecv.at[pl.ds(first, PT - first)], o_rs.at[tile])
        cols = slice(tile * PT * 16, (tile + 1) * PT * 16)
        for gq in range(2):
            for j in range(JB):
                back = orecv[tile * PT:(tile + 1) * PT, j, gq * 16:(gq + 1) * 16, :].reshape(PT * 16, HD)
                new = dot(ret[j, :, cols], back)
                parts[gq] = new if parts[gq] is None else parts[gq] + new
    for g in range(GR):
        rows = slice(g * QD, (g + 1) * QD)
        mixed = own_o[rows, :]
        for t in range(TOP):
            first = (g % 4 * TOP + t) * QD
            mixed += weight[t, rows, :] * parts[g // 4][first:first + QD]
        att_ref[0, :, g * HD:(g + 1) * HD] = mixed.astype(BF16)

    w_load.wait()
    att = att_ref[0]

    def over_y(c):
        wait_for(r_recv.at[c], r_rs.at[c])
        both = r_stage[core, c].astype(F32) + r_recv[c].astype(F32)
        y_send[c] = both.astype(BF16)

        for i in (2, 1, 3):
            to = along_y(i)
            send(y_send.at[c, to], y_recv.at[c, i], y_ss, y_rs.at[c], {"kvh": 2 * to + core})

    for c in range(CHUNKS):
        part = dot(att, wbuf[:, c * CW:(c + 1) * CW])
        for k in range(2 * NY):
            rows = part[k * 8:(k + 1) * 8]
            both = jnp.concatenate([rows[:, :CW // 2], rows[:, CW // 2:]], axis=0)
            r_stage[k % 2, c, k // 2] = both.astype(BF16)
        send(r_stage.at[1 - core, c], r_recv.at[c], r_ss, r_rs.at[c], sibling)
        if c > 0:
            over_y(c - 1)
    over_y(CHUNKS - 1)
    for c in range(CHUNKS):
        wait_for(y_recv.at[c, pl.ds(1, NY - 1)], y_rs.at[c])
        total = y_send[c, y].astype(F32)
        for i in range(1, NY):
            total += y_recv[c, i].astype(F32)
        proj_ref[:, c * CW:c * CW + CW // 2] = total[:8].astype(BF16)
        proj_ref[:, c * CW + CW // 2:(c + 1) * CW] = total[8:].astype(BF16)

    for buf, sem in ((qsend, q_ss), (osend, o_ss), (lsend, l_ss)):
        part = buf.at[pl.ds(0, N - 1)]
        wait_for(part, sem)
    part = sp.at[0, :, pl.ds(0, (NZ - 1) * QD), :]
    wait_for(part, a_ss)
    part = sp.at[pl.ds(0, NX - 1)]
    wait_for(part, b_ss)
    wait_for(r_recv, r_ss)
    wait_for(y_recv.at[:, pl.ds(1, NY - 1)], y_ss)


def on_device(queries, span_kv, cache_kv, choices, block_home, out_weight):
    vmem = pl.BlockSpec(memory_space=pltpu.VMEM)
    hbm = pl.BlockSpec(memory_space=pl.ANY)
    dma = pltpu.SemaphoreType.DMA
    attended, projected = pl.pallas_call(
        kernel,
        out_shape=(
            pltpu.VMEM((1, QD, GR * HD), BF16),
            pltpu.VMEM((8, COLS), BF16),
        ),
        in_specs=[hbm] * 6,
        out_specs=(vmem, vmem),
        scratch_shapes=[
            pltpu.VMEM((1, QD, GR * HD), BF16),
            pltpu.VMEM((TOP, 1, 128), jnp.int32),
            pltpu.VMEM((1, NB), jnp.int32),
            pltpu.VMEM((JB, BL, HD), BF16),
            pltpu.VMEM((JB, BL, HD), BF16),
            pltpu.VMEM((GR * HD, COLS), BF16),
            pltpu.VMEM((N, JB, 32, HD), BF16),
            pltpu.VMEM((N, JB, 32, HD), BF16),
            pltpu.VMEM((N, JB, 32, HD), BF16),
            pltpu.VMEM((N, JB, 32, HD), BF16),
            pltpu.VMEM((N, 1, 128), F32),
            pltpu.VMEM((N, 1, 128), F32),
            pltpu.VMEM((NX, 2, NZ * QD, HD), BF16),
            pltpu.VMEM((JB, RT, BL), F32),
            pltpu.VMEM((JB, 4 * TOP * QD, N * 16), BF16),
            pltpu.VMEM((GR * QD, HD), F32),
            pltpu.VMEM((2, GR * QD, HD), F32),
            pltpu.VMEM((TOP, GR * QD, HD), F32),
            pltpu.VMEM((2, CHUNKS, NY, 16, CW // 2), BF16),
            pltpu.VMEM((CHUNKS, NY, 16, CW // 2), BF16),
            pltpu.VMEM((CHUNKS, NY, 16, CW // 2), BF16),
            pltpu.VMEM((CHUNKS, NY, 16, CW // 2), BF16),
            dma((4,)),
            dma((4,)),
            dma,
            dma,
            dma((TILES,)),
            dma,
            dma((TILES,)),
            dma, dma, dma, dma, dma, dma,
            dma((NX,)),
            dma,
            dma((CHUNKS,)),
            dma,
            dma((CHUNKS,)),
        ],
        compiler_params=pltpu.CompilerParams(
            collective_id=0, has_side_effects=True, vmem_limit_bytes=56 * 2**20
        ),
    )(
        queries,
        span_kv,
        cache_kv,
        jnp.transpose(choices, (2, 0, 1)),
        block_home.reshape(1, NB),
        out_weight,
    )
    return attended, projected


def solution(mesh):
    return jax.shard_map(
        on_device,
        mesh=mesh,
        in_specs=(
            P("kvh", "ctx", None),
            P(None, "kvh", "ctx", None),
            P(None, "kvh", "ctx", None),
            P("kvh", None, None),
            P(),
            P("kvh", None),
        ),
        out_specs=(P("kvh", "ctx", None), P(("ctx", "kvh"), None)),
        check_vma=False,
    )
```
